512 devices in a mesh: dp: 32 (over x, y), seq: 16 (over z, core).
Axes of the slice: x: 4, y: 8, z: 8, core: 2. Of those that a mesh axis runs over, the one named last changes fastest.
Arguments:
- queries: bfloat16 [32, 2048, 2048], P('dp', 'seq'), may hold values from -6 to 6
- key_rows: bfloat16 [32, 2048, 2048], P('dp', 'seq'), may hold values from -6 to 6
- value_rows: bfloat16 [32, 2048, 2048], P('dp', 'seq'), may hold values from -6 to 6
- out_grad: bfloat16 [32, 2048, 2048], P('dp', 'seq'), may hold values from -6 to 6
- norm_gain: float32 [2048], P('dp'), may hold values from 0.25 to 1.75
- doc_starts: int32 [32, 8], P('dp'), may hold values from 0 to 2047, as said below
Outputs:
- attended: bfloat16 [32, 2048, 2048], P('dp', 'seq')
- query_grad: bfloat16 [32, 2048, 2048], P('dp', 'seq')
- key_grad: bfloat16 [32, 2048, 2048], P('dp', 'seq')
- value_grad: bfloat16 [32, 2048, 2048], P('dp', 'seq')
- gain_grad: float32 [2048], P('dp')
The draws below stay inside these ranges and needn't reach their ends.
Inputs may be any that keep to these rules, and one draw needn't show every extreme that they name: `doc_starts`: each row begins with 0 and rises strictly.
All inputs are finite; a program needn't handle non-finite values.
Results may differ from the reference program's by a relative error of at most 0.011.
Values sent between devices are 32-bit elements; how exact they have to be, the bound alone decides.
No kernel may reach another device: no remote copies, remote signals or barrier semaphores. Data moves between devices by JAX's collectives and lax.ppermute only.
A program may use at most 128 MiB of HBM per device.

```python
import math
import jax
import jax.numpy as jnp
from jax import lax

HEADS = 16
FEAT = 128
TOK_DEV = 128
DOCS = 8
SEQS = 32
LENGTH = 2048
WIDTH = 2048


def draw_doc_starts(key, part):
    key = jax.random.fold_in(key, 7)
    row_base, order_key = jax.random.split(key)
    keys = jax.random.split(row_base, SEQS)
    order = jax.random.permutation(order_key, SEQS)
    tail_rows = order < (SEQS + 1) // 2

    def one_row(row_key, in_tail):
        spread_key, tail_key = jax.random.split(row_key)
        spread = jax.random.choice(spread_key, LENGTH - 1, (DOCS - 1,), replace=False) + 1
        tail = jax.random.choice(tail_key, TOK_DEV - 1, (DOCS - 1,), replace=False) + (LENGTH - TOK_DEV + 1)
        picks = jnp.where(in_tail, tail.astype(jnp.int32), spread.astype(jnp.int32))
        picks = jnp.sort(picks)
        return jnp.concatenate([jnp.zeros((1,), jnp.int32), picks])
    return jax.vmap(one_row)(keys, tail_rows).astype(jnp.int32)


def shard_levels(rng, dims, cuts, least, largest):
    factor_of = 1.0
    for axis_at, parts in cuts:
        steps = jax.random.uniform(jax.random.fold_in(jax.random.fold_in(rng, 6), axis_at), (parts,), jnp.float32, least / len(cuts), largest / len(cuts))
        factor_of = factor_of * jnp.repeat(jnp.exp(steps), dims[axis_at] // parts).reshape((-1,) + (1,) * (len(dims) - 1 - axis_at))
    return factor_of


def centred(own_key, dims, deviation, reach, shards=(), kind=jnp.bfloat16):
    drawn = jax.random.normal(own_key, dims, jnp.float32) * deviation
    if len(shards) > 0:
        drawn = shard_levels(own_key, dims, shards, -0.22, 0.18) * drawn
    return jnp.clip(drawn, min=-reach, max=reach).astype(kind)


def setup_inputs(seed: int = 0) -> dict:
    arg_keys = jax.random.split(jax.random.key(seed), 7)
    queries = centred(arg_keys[0], (SEQS, LENGTH, WIDTH), 1.0, 6.0, ((0, 32), (1, 16)))
    key_rows = centred(arg_keys[1], (SEQS, LENGTH, WIDTH), 1.0, 6.0, ((0, 32), (1, 16)))
    value_rows = centred(arg_keys[2], (SEQS, LENGTH, WIDTH), 1.0, 6.0, ((0, 32), (1, 16)))
    out_grad = centred(arg_keys[3], (SEQS, LENGTH, WIDTH), 1.0, 6.0, ((0, 32), (1, 16)))
    norm_gain = jnp.clip(1.0 + 0.15 * jax.random.normal(arg_keys[4], (WIDTH,), jnp.float32), 0.25, 1.75)
    doc_starts = draw_doc_starts(jax.random.fold_in(arg_keys[6], 71), 0)
    return dict(queries=queries, key_rows=key_rows, value_rows=value_rows, out_grad=out_grad, norm_gain=norm_gain, doc_starts=doc_starts)


EPS = 1e-06

def features(x):
    return jnp.where(x > 0, x + 1.0, jnp.exp(jnp.minimum(x, 0.0)))

def slope(x):
    return jnp.where(x > 0, 1.0, jnp.exp(jnp.minimum(x, 0.0)))

def rounded(x):
    return lax.optimization_barrier(x.astype(jnp.bfloat16)).astype(jnp.float32)

def one_sequence(args):
    qin, kin, vin, grad_in, starts, gain = args
    blocks = LENGTH // TOK_DEV
    shape = (blocks, TOK_DEV, HEADS, FEAT)
    pos = jnp.arange(LENGTH, dtype=jnp.int32).reshape(blocks, TOK_DEV)
    docs = lax.optimization_barrier(jnp.sum((starts[None, None, :] <= pos[..., None]).astype(jnp.int32), -1))
    first = jnp.arange(blocks, dtype=jnp.int32) * TOK_DEV
    before = lax.optimization_barrier(jnp.sum((starts[None, :] <= (first - 1)[:, None]).astype(jnp.int32), -1))
    last_doc = docs[:, -1]
    cin = (docs == before[:, None]).astype(jnp.float32)[..., None, None]
    eout = (docs == last_doc[:, None]).astype(jnp.float32)[..., None, None]
    passes = (last_doc == before).astype(jnp.float32)[:, None, None, None]
    tri = jnp.arange(TOK_DEV)[:, None] >= jnp.arange(TOK_DEV)[None, :]
    mask = (tri[None] & (docs[:, :, None] == docs[:, None, :])).astype(jnp.float32)[:, None]
    q32 = qin.astype(jnp.float32).reshape(shape)
    k32 = kin.astype(jnp.float32).reshape(shape)
    v32 = vin.astype(jnp.float32).reshape(shape)
    qb = rounded(features(q32))
    kb = rounded(features(k32))
    scores = rounded(jnp.einsum('nthf,nshf->nhts', qb, kb) * mask)
    intra = jnp.einsum('nhts,nshf->nthf', scores, v32)
    local = jnp.einsum('nthf,nthe->nhfe', kb * eout, v32)

    def fwd(carry, item):
        part, flag = item
        return (part + flag * carry, carry)
    zero = jnp.zeros((HEADS, FEAT, FEAT), jnp.float32)
    _, incoming = lax.scan(fwd, zero, (local, passes))
    inb = rounded(incoming)
    num = intra + jnp.einsum('nthf,nhfe->nthe', qb, inb) * cin
    recip = lax.rsqrt(lax.optimization_barrier(jnp.mean(num * num, -1, keepdims=True)) + EPS)
    normed = num * recip
    gains = gain.reshape(HEADS, FEAT)
    attended = (normed * gains).astype(jnp.bfloat16)
    dy = grad_in.astype(jnp.float32).reshape(shape)
    upper = dy * gains
    dn = rounded(recip * upper - normed * recip * lax.optimization_barrier(jnp.mean(upper * normed, -1, keepdims=True)))
    gterm = lax.optimization_barrier(jnp.sum(dy * normed, axis=(0, 1)))
    dscores = rounded(jnp.einsum('nthf,nshf->nhts', dn, v32) * mask)
    state_grad = jnp.einsum('nthf,nthe->nhfe', qb, dn * cin)

    def bwd(carry, item):
        part, flag = item
        return (part + flag * carry, carry)
    _, outgoing = lax.scan(bwd, zero, (state_grad, passes), reverse=True)
    outb = rounded(outgoing)
    dq = jnp.einsum('nhts,nshf->nthf', dscores, kb) + jnp.einsum('nthe,nhfe->nthf', dn, inb) * cin
    dk = jnp.einsum('nhts,nthf->nshf', dscores, qb) + jnp.einsum('nthe,nhfe->nthf', v32, outb) * eout
    dv = jnp.einsum('nhts,nthf->nshf', scores, dn) + jnp.einsum('nthf,nhfe->nthe', kb, outb) * eout
    dq = dq * slope(q32)
    dk = dk * slope(k32)
    flat = (LENGTH, HEADS * FEAT)
    return (attended.reshape(flat), dq.astype(jnp.bfloat16).reshape(flat), dk.astype(jnp.bfloat16).reshape(flat), dv.astype(jnp.bfloat16).reshape(flat), gterm)

def reference(queries, key_rows, value_rows, out_grad, norm_gain, doc_starts):
    gains = jnp.broadcast_to(norm_gain[None], (SEQS, HEADS * FEAT))
    attended, query_grad, key_grad, value_grad, terms = lax.map(one_sequence, (queries, key_rows, value_rows, out_grad, doc_starts, gains))
    gain_grad = lax.optimization_barrier(jnp.sum(terms, axis=0)).reshape(HEADS * FEAT) / math.sqrt(SEQS * LENGTH)
    return (attended, query_grad, key_grad, value_grad, gain_grad)
```

```python
import math

import jax
import jax.numpy as jnp
from jax import lax
from jax.experimental import pallas as pl
from jax.experimental.pallas import tpu as pltpu
from jax.sharding import PartitionSpec as P

HEADS = 16
FEAT = 128
TOK = 128
HALF = HEADS // 2
CHIPS = 8
DOCS = 8
EPS = 1e-06
F32 = jnp.float32
BF16 = jnp.bfloat16

VM = pl.BlockSpec(memory_space=pltpu.VMEM)
SM = pl.BlockSpec(memory_space=pltpu.SMEM)


def call(body, outs, n_in, flops=0, nbytes=0, trans=0):
    return pl.pallas_call(
        body,
        out_shape=[jax.ShapeDtypeStruct(s, d) for s, d in outs],
        in_specs=[SM] + [VM] * (n_in - 1),
        out_specs=[VM] * len(outs),
        compiler_params=pltpu.CompilerParams(vmem_limit_bytes=24 * 1024 * 1024),
        cost_estimate=pl.CostEstimate(
            flops=flops, bytes_accessed=nbytes, transcendentals=trans
        ),
    )


def doc_at(starts, p):
    total = jnp.int32(0)
    for j in range(DOCS):
        total = total + (starts[0, j] <= p).astype(jnp.int32)
    return total


def docs_of(starts, pos):
    total = jnp.zeros(pos.shape, jnp.int32)
    for j in range(DOCS):
        total = total + (starts[0, j] <= pos).astype(jnp.int32)
    return total


def place():
    idx = lax.axis_index("seq")
    return idx, lax.rem(idx, 2)


def row_pos(idx):
    return idx * TOK + lax.broadcasted_iota(jnp.int32, (TOK, FEAT), 0)


def enters(starts, idx):
    return docs_of(starts, row_pos(idx)) == doc_at(starts, idx * TOK - 1)


def leaves(starts, idx):
    return docs_of(starts, row_pos(idx)) == doc_at(starts, idx * TOK + TOK - 1)


def mask_of(starts, idx):
    rows = row_pos(idx)
    cols = idx * TOK + lax.broadcasted_iota(jnp.int32, (TOK, TOK), 1)
    return (rows >= cols) & (docs_of(starts, rows) == docs_of(starts, cols))


def carry_of(starts, idx):
    return (doc_at(starts, idx * TOK - 1) == doc_at(starts, idx * TOK + TOK - 1)).astype(F32)


def chip_carry(starts, z):
    first = z * 2 * TOK
    return (doc_at(starts, first - 1) == doc_at(starts, first + 2 * TOK - 1)).astype(F32)


def phi(x):
    return jnp.where(x > 0, x + 1.0, jnp.exp(jnp.minimum(x, 0.0)))


def slope(x):
    return jnp.where(x > 0, 1.0, jnp.exp(jnp.minimum(x, 0.0)))


def dot(a, b, ca, cb):
    return lax.dot_general(a, b, (((ca,), (cb,)), ((), ())), preferred_element_type=F32)


def cols(h):
    return pl.ds(pl.multiple_of(h * FEAT, FEAT), FEAT)


def state_body(starts, k, v, keep, give):
    idx, core = place()
    last = leaves(starts, idx)
    for j in range(HALF):
        for out, side in ((keep, core), (give, 1 - core)):
            at = cols(side * HALF + j)
            kf = jnp.where(last, phi(k[:, at].astype(F32)), 0.0).astype(BF16)
            out[j] = dot(kf, v[:, at], 0, 0)


def join_body(starts, keep, recv, out):
    idx, core = place()
    later = carry_of(starts, idx - core + 1)
    mine = jnp.where(core == 0, later, 1.0)
    theirs = jnp.where(core == 0, 1.0, later)
    for j in range(HALF):
        out[j] = mine * keep[j] + theirs * recv[j]


def join_back_body(starts, keep, recv, out):
    idx, core = place()
    earlier = carry_of(starts, idx - core)
    mine = jnp.where(core == 0, 1.0, earlier)
    theirs = jnp.where(core == 0, earlier, 1.0)
    for j in range(HALF):
        out[j] = mine * keep[j] + theirs * recv[j]


def scan_body(starts, parts, out):
    total = jnp.zeros((FEAT, FEAT), F32)
    for z in range(CHIPS):
        out[z] = total
        if z < CHIPS - 1:
            total = parts[z] + chip_carry(starts, z) * total


def scan_back_body(starts, parts, terms, out):
    total = jnp.zeros((FEAT, FEAT), F32)
    gsum = jnp.broadcast_to(jnp.sum(terms[...], axis=0, keepdims=True), (8, FEAT))
    for z in reversed(range(CHIPS)):
        out[z, :FEAT] = total
        out[z, FEAT:] = gsum
        if z > 0:
            total = parts[z] + chip_carry(starts, z) * total


def give_body(starts, keep, coming, out):
    idx, core = place()
    flag = carry_of(starts, idx - core)
    a = jnp.where(core == 0, 1.0, 0.0)
    b = jnp.where(core == 0, flag, 1.0)
    for j in range(HALF):
        out[j] = a * keep[j] + b * coming[j]


def give_back_body(starts, keep, coming, out):
    idx, core = place()
    flag = carry_of(starts, idx - core + 1)
    a = jnp.where(core == 0, 0.0, 1.0)
    b = jnp.where(core == 0, 1.0, flag)
    gsum = jnp.zeros((8, FEAT), F32)
    for j in range(HALF):
        out[j * FEAT : (j + 1) * FEAT] = a * keep[j] + b * coming[j, :FEAT]
        gsum = gsum + coming[j, FEAT:]
    out[HALF * FEAT :] = gsum


def local_body(starts, q, k, v, qf_out, kf_out, scores_out, intra_out):
    idx, _ = place()
    mask = mask_of(starts, idx)
    for h in range(HEADS):
        at = slice(h * FEAT, (h + 1) * FEAT)
        qf = phi(q[:, at].astype(F32)).astype(BF16)
        kf = phi(k[:, at].astype(F32)).astype(BF16)
        qf_out[:, at] = qf
        kf_out[:, at] = kf
        scores = jnp.where(mask, dot(qf, kf, 1, 1), 0.0).astype(BF16)
        scores_out[:, at] = scores
        intra_out[:, at] = dot(scores, v[:, at], 1, 0)


def norm_body(
    starts, qf, intra, dy, gains, coming, theirs, ready,
    att, dn_out, inb_out, keep, give, terms,
):
    idx, core = place()
    cin = enters(starts, idx)
    flag = carry_of(starts, idx - core)
    a = jnp.where(core == 0, 0.0, 1.0)
    b = jnp.where(core == 0, 1.0, flag)
    for j in range(HALF):
        for side, state in ((core, keep), (1 - core, give)):
            h = side * HALF + j
            at = cols(h)
            incoming = a * theirs[j] + b * coming[j] if state is keep else ready[j]
            inb = incoming.astype(BF16)
            inb_out[h] = inb
            qh = qf[:, at]
            num = intra[:, at] + jnp.where(cin, dot(qh, inb, 1, 0), 0.0)
            recip = lax.rsqrt(jnp.mean(num * num, -1, keepdims=True) + EPS)
            normed = num * recip
            gain = gains[pl.ds(2 * h, 1), :] + gains[pl.ds(2 * h + 1, 1), :]
            att[:, at] = (normed * gain).astype(BF16)
            grad = dy[:, at].astype(F32)
            upper = grad * gain
            mean = jnp.mean(upper * normed, -1, keepdims=True)
            dn = (recip * upper - normed * recip * mean).astype(BF16)
            dn_out[:, at] = dn
            term = jnp.sum(grad * normed, axis=0, keepdims=True)
            terms[pl.ds(2 * h, 1), :] = term
            terms[pl.ds(2 * h + 1, 1), :] = term
            masked = jnp.where(cin, dn, jnp.zeros_like(dn))
            state[j] = dot(qh, masked, 0, 0)


def grads_body(starts, q, v, qf, kf, scores, dn, inb, dq_out, dk_part, dv_part):
    idx, _ = place()
    mask = mask_of(starts, idx)
    cin = enters(starts, idx)
    for h in range(HEADS):
        at = slice(h * FEAT, (h + 1) * FEAT)
        dnh = dn[:, at]
        dscores = jnp.where(mask, dot(dnh, v[:, at], 1, 1), 0.0).astype(BF16)
        dq = dot(dscores, kf[:, at], 1, 0) + jnp.where(cin, dot(dnh, inb[h], 1, 1), 0.0)
        dq_out[:, at] = (dq * slope(q[:, at].astype(F32))).astype(BF16)
        dk_part[:, at] = dot(dscores, qf[:, at], 0, 0)
        dv_part[:, at] = dot(scores[:, at], dnh, 0, 0)


def last_body(
    starts, k, v, kf, dk_part, dv_part, theirs, coming, ready,
    dk_out, dv_out, gain_out,
):
    idx, core = place()
    last = leaves(starts, idx)
    flag = carry_of(starts, idx - core + 1)
    a = jnp.where(core == 0, 1.0, 0.0)
    b = jnp.where(core == 0, flag, 1.0)
    gsum = ready[HALF * FEAT :]
    for j in range(HALF):
        gsum = gsum + coming[j, FEAT:]
        for mine, side in ((True, core), (False, 1 - core)):
            at = cols(side * HALF + j)
            if mine:
                outgoing = a * theirs[j] + b * coming[j, :FEAT]
            else:
                outgoing = ready[j * FEAT : (j + 1) * FEAT]
            outb = outgoing.astype(BF16)
            dk = dk_part[:, at] + jnp.where(last, dot(v[:, at], outb, 1, 1), 0.0)
            dk_out[:, at] = (dk * slope(k[:, at].astype(F32))).astype(BF16)
            dv = dv_part[:, at] + jnp.where(last, dot(kf[:, at], outb, 1, 0), 0.0)
            dv_out[:, at] = dv.astype(BF16)
    half = lax.rem(lax.axis_index("dp"), 2)
    total = gsum[:1] * (1.0 / math.sqrt(32 * 2048))
    gain_out[...] = jnp.where(half == 0, total[:, :64], total[:, 64:])


def shards(queries, key_rows, value_rows, out_grad, norm_gain, doc_starts):
    q, k, v, dy = (a.reshape(TOK, HEADS * FEAT) for a in (queries, key_rows, value_rows, out_grad))
    starts = doc_starts
    swap = [(i, i ^ 1) for i in range(2 * CHIPS)]
    zgroups = [[2 * z + c for z in range(CHIPS)] for c in range(2)]
    wide = (TOK, HEADS * FEAT)
    half_states = (HALF, FEAT, FEAT)
    mm = 2 * TOK * FEAT * FEAT

    def other(x):
        return lax.ppermute(x, "seq", swap)

    def across(x):
        return lax.all_to_all(x, "seq", 0, 0, axis_index_groups=zgroups, tiled=True)

    parity = lax.rem(lax.axis_index("dp"), 2)
    row = jnp.where(
        jnp.arange(FEAT) // 64 == parity, jnp.concatenate([norm_gain, norm_gain]), 0.0
    )
    gains = lax.all_to_all(jnp.broadcast_to(row[None], (32, FEAT)), "dp", 0, 0, tiled=True)

    keep1, give1 = call(
        state_body, [(half_states, F32)] * 2, 3, 16 * mm, 2 << 20, 1 << 18
    )(starts, k, v)
    recv1 = other(give1)
    (chip,) = call(join_body, [(half_states, F32)], 3, 1 << 18, 3 << 19)(starts, keep1, recv1)
    parts = across(chip)
    qf, kf, scores, intra = call(
        local_body, [(wide, BF16)] * 3 + [(wide, F32)], 4, 32 * mm, 4 << 20, 1 << 19
    )(starts, q, k, v)
    (prefix,) = call(scan_body, [(half_states, F32)], 2, 1 << 18, 1 << 20)(starts, parts)
    coming = across(prefix)
    (send2,) = call(give_body, [(half_states, F32)], 3, 1 << 18, 3 << 19)(starts, keep1, coming)
    ready = other(send2)
    att, dn, inb, keep3, give3, terms = call(
        norm_body,
        [(wide, BF16), (wide, BF16), ((HEADS, FEAT, FEAT), BF16)]
        + [(half_states, F32)] * 2
        + [((32, FEAT), F32)],
        8, 32 * mm, 5 << 20, 1 << 15,
    )(starts, qf, intra, dy, gains, coming, recv1, ready)
    gathered = lax.all_to_all(terms, "dp", 0, 0, tiled=True)
    recv3 = other(give3)
    (chip3,) = call(join_back_body, [(half_states, F32)], 3, 1 << 18, 3 << 19)(starts, keep3, recv3)
    parts3 = across(chip3)
    dq, dk_part, dv_part = call(
        grads_body, [(wide, BF16), (wide, F32), (wide, F32)], 8, 80 * mm, 7 << 20, 1 << 18
    )(starts, q, v, qf, kf, scores, dn, inb)
    (suffix,) = call(
        scan_back_body, [((CHIPS, FEAT + 8, FEAT), F32)], 3, 1 << 18, 1 << 20
    )(starts, parts3, gathered)
    coming4 = across(suffix)
    (send4,) = call(
        give_back_body, [((HALF * FEAT + 8, FEAT), F32)], 3, 1 << 18, 3 << 19
    )(starts, keep3, coming4)
    ready4 = other(send4)
    dk, dv, gain_grad = call(
        last_body, [(wide, BF16)] * 2 + [((1, 64), F32)], 9, 32 * mm, 5 << 20, 1 << 18
    )(starts, k, v, kf, dk_part, dv_part, recv3, coming4, ready4)
    full = (1, TOK, HEADS * FEAT)
    return (
        att.reshape(full),
        dq.reshape(full),
        dk.reshape(full),
        dv.reshape(full),
        gain_grad.reshape(64),
    )


def solution(mesh):
    rows = P("dp", "seq", None)
    return jax.shard_map(
        shards,
        mesh=mesh,
        in_specs=(rows, rows, rows, rows, P("dp"), P("dp", None)),
        out_specs=(rows, rows, rows, rows, P("dp")),
        check_vma=False,
    )
```

```python
import math

import jax
import jax.numpy as jnp
from jax import lax
from jax.experimental import pallas as pl
from jax.experimental.pallas import tpu as pltpu
from jax.sharding import PartitionSpec as P

HEADS = 16
FEAT = 128
TOK = 128
HALF = HEADS // 2
CHIPS = 8
DOCS = 8
EPS = 1e-06
F32 = jnp.float32
BF16 = jnp.bfloat16

VM = pl.BlockSpec(memory_space=pltpu.VMEM)
SM = pl.BlockSpec(memory_space=pltpu.SMEM)


def call(body, outs, n_in, flops=0, nbytes=0, trans=0):
    return pl.pallas_call(
        body,
        out_shape=[jax.ShapeDtypeStruct(s, d) for s, d in outs],
        in_specs=[SM] + [VM] * (n_in - 1),
        out_specs=[VM] * len(outs),
        compiler_params=pltpu.CompilerParams(vmem_limit_bytes=24 * 1024 * 1024),
        cost_estimate=pl.CostEstimate(
            flops=flops, bytes_accessed=nbytes, transcendentals=trans
        ),
    )


def doc_at(starts, p):
    total = jnp.int32(0)
    for j in range(DOCS):
        total = total + (starts[0, j] <= p).astype(jnp.int32)
    return total


def docs_of(starts, pos):
    total = jnp.zeros(pos.shape, jnp.int32)
    for j in range(DOCS):
        total = total + (starts[0, j] <= pos).astype(jnp.int32)
    return total


def place():
    idx = lax.axis_index("seq")
    return idx, lax.rem(idx, 2)


def row_pos(idx):
    return idx * TOK + lax.broadcasted_iota(jnp.int32, (TOK, FEAT), 0)


def enters(starts, idx):
    return docs_of(starts, row_pos(idx)) == doc_at(starts, idx * TOK - 1)


def leaves(starts, idx):
    return docs_of(starts, row_pos(idx)) == doc_at(starts, idx * TOK + TOK - 1)


def mask_of(starts, idx):
    rows = row_pos(idx)
    cols = idx * TOK + lax.broadcasted_iota(jnp.int32, (TOK, TOK), 1)
    return (rows >= cols) & (docs_of(starts, rows) == docs_of(starts, cols))


def carry_of(starts, idx):
    return (doc_at(starts, idx * TOK - 1) == doc_at(starts, idx * TOK + TOK - 1)).astype(F32)


def chip_carry(starts, z):
    first = z * 2 * TOK
    return (doc_at(starts, first - 1) == doc_at(starts, first + 2 * TOK - 1)).astype(F32)


def phi(x):
    return jnp.where(x > 0, x + 1.0, jnp.exp(jnp.minimum(x, 0.0)))


def slope(x):
    return jnp.where(x > 0, 1.0, jnp.exp(jnp.minimum(x, 0.0)))


def dot(a, b, ca, cb):
    return lax.dot_general(a, b, (((ca,), (cb,)), ((), ())), preferred_element_type=F32)


def cols(h):
    return pl.ds(pl.multiple_of(h * FEAT, FEAT), FEAT)


def state_body(starts, k, v, keep, give):
    idx, core = place()
    last = leaves(starts, idx)
    for j in range(HALF):
        for out, side in ((keep, core), (give, 1 - core)):
            at = cols(side * HALF + j)
            kf = jnp.where(last, phi(k[:, at].astype(F32)), 0.0).astype(BF16)
            out[j] = dot(kf, v[:, at], 0, 0)


def join_body(starts, keep, recv, out):
    idx, core = place()
    later = carry_of(starts, idx - core + 1)
    mine = jnp.where(core == 0, later, 1.0)
    theirs = jnp.where(core == 0, 1.0, later)
    for j in range(HALF):
        out[j] = mine * keep[j] + theirs * recv[j]


def join_back_body(starts, keep, recv, out):
    idx, core = place()
    earlier = carry_of(starts, idx - core)
    mine = jnp.where(core == 0, 1.0, earlier)
    theirs = jnp.where(core == 0, earlier, 1.0)
    for j in range(HALF):
        out[j] = mine * keep[j] + theirs * recv[j]


def scan_body(starts, parts, out):
    total = jnp.zeros((FEAT, FEAT), F32)
    for z in range(CHIPS):
        out[z] = total
        if z < CHIPS - 1:
            total = parts[z] + chip_carry(starts, z) * total


def scan_back_body(starts, parts, terms, out):
    total = jnp.zeros((FEAT, FEAT), F32)
    gsum = jnp.broadcast_to(jnp.sum(terms[...], axis=0, keepdims=True), (8, FEAT))
    for z in reversed(range(CHIPS)):
        out[z, :FEAT] = total
        out[z, FEAT:] = gsum
        if z > 0:
            total = parts[z] + chip_carry(starts, z) * total


def give_body(starts, keep, coming, out):
    idx, core = place()
    flag = carry_of(starts, idx - core)
    a = jnp.where(core == 0, 1.0, 0.0)
    b = jnp.where(core == 0, flag, 1.0)
    for j in range(HALF):
        out[j] = a * keep[j] + b * coming[j]


def give_back_body(starts, keep, coming, out):
    idx, core = place()
    flag = carry_of(starts, idx - core + 1)
    a = jnp.where(core == 0, 0.0, 1.0)
    b = jnp.where(core == 0, 1.0, flag)
    gsum = jnp.zeros((8, FEAT), F32)
    for j in range(HALF):
        out[j * FEAT : (j + 1) * FEAT] = a * keep[j] + b * coming[j, :FEAT]
        gsum = gsum + coming[j, FEAT:]
    out[HALF * FEAT :] = gsum


def local_body(starts, q, k, v, qf_out, kf_out, scores_out, intra_out):
    idx, _ = place()
    mask = mask_of(starts, idx)
    for h in range(HEADS):
        at = slice(h * FEAT, (h + 1) * FEAT)
        qf = phi(q[:, at].astype(F32)).astype(BF16)
        kf = phi(k[:, at].astype(F32)).astype(BF16)
        qf_out[:, at] = qf
        kf_out[:, at] = kf
        scores = jnp.where(mask, dot(qf, kf, 1, 1), 0.0).astype(BF16)
        scores_out[:, at] = scores
        intra_out[:, at] = dot(scores, v[:, at], 1, 0)


def norm_body(
    starts, qf, intra, dy, gains, coming, theirs, ready,
    att, dn_out, inb_out, keep, give, terms,
):
    idx, core = place()
    cin = enters(starts, idx)
    flag = carry_of(starts, idx - core)
    a = jnp.where(core == 0, 0.0, 1.0)
    b = jnp.where(core == 0, 1.0, flag)
    for j in range(HALF):
        for side, state in ((core, keep), (1 - core, give)):
            h = side * HALF + j
            at = cols(h)
            incoming = a * theirs[j] + b * coming[j] if state is keep else ready[j]
            inb = incoming.astype(BF16)
            inb_out[h] = inb
            qh = qf[:, at]
            num = intra[:, at] + jnp.where(cin, dot(qh, inb, 1, 0), 0.0)
            recip = lax.rsqrt(jnp.mean(num * num, -1, keepdims=True) + EPS)
            normed = num * recip
            gain = gains[pl.ds(2 * h, 1), :] + gains[pl.ds(2 * h + 1, 1), :]
            att[:, at] = (normed * gain).astype(BF16)
            grad = dy[:, at].astype(F32)
            upper = grad * gain
            mean = jnp.mean(upper * normed, -1, keepdims=True)
            dn = (recip * upper - normed * recip * mean).astype(BF16)
            dn_out[:, at] = dn
            term = jnp.sum(grad * normed, axis=0, keepdims=True)
            terms[pl.ds(2 * h, 1), :] = term
            terms[pl.ds(2 * h + 1, 1), :] = term
            masked = jnp.where(cin, dn, jnp.zeros_like(dn))
            state[j] = dot(qh, masked, 0, 0)


def grads_body(starts, q, v, qf, kf, scores, dn, inb, dq_out, dk_part, dv_part):
    idx, _ = place()
    mask = mask_of(starts, idx)
    cin = enters(starts, idx)
    for h in range(HEADS):
        at = slice(h * FEAT, (h + 1) * FEAT)
        dnh = dn[:, at]
        dscores = jnp.where(mask, dot(dnh, v[:, at], 1, 1), 0.0).astype(BF16)
        dq = dot(dscores, kf[:, at], 1, 0) + jnp.where(cin, dot(dnh, inb[h], 1, 1), 0.0)
        dq_out[:, at] = (dq * slope(q[:, at].astype(F32))).astype(BF16)
        dk_part[:, at] = dot(dscores, qf[:, at], 0, 0)
        dv_part[:, at] = dot(scores[:, at], dnh, 0, 0)


def last_body(
    starts, k, v, kf, dk_part, dv_part, theirs, coming, ready,
    dk_out, dv_out, gain_out,
):
    idx, core = place()
    last = leaves(starts, idx)
    flag = carry_of(starts, idx - core + 1)
    a = jnp.where(core == 0, 1.0, 0.0)
    b = jnp.where(core == 0, flag, 1.0)
    gsum = ready[HALF * FEAT :]
    for j in range(HALF):
        gsum = gsum + coming[j, FEAT:]
        for mine, side in ((True, core), (False, 1 - core)):
            at = cols(side * HALF + j)
            if mine:
                outgoing = a * theirs[j] + b * coming[j, :FEAT]
            else:
                outgoing = ready[j * FEAT : (j + 1) * FEAT]
            outb = outgoing.astype(BF16)
            dk = dk_part[:, at] + jnp.where(last, dot(v[:, at], outb, 1, 1), 0.0)
            dk_out[:, at] = (dk * slope(k[:, at].astype(F32))).astype(BF16)
            dv = dv_part[:, at] + jnp.where(last, dot(kf[:, at], outb, 1, 0), 0.0)
            dv_out[:, at] = dv.astype(BF16)
    half = lax.rem(lax.axis_index("dp"), 2)
    total = gsum[:1] * (1.0 / math.sqrt(32 * 2048))
    gain_out[...] = jnp.where(half == 0, total[:, :64], total[:, 64:])


def shards(queries, key_rows, value_rows, out_grad, norm_gain, doc_starts):
    q, k, v, dy = (a.reshape(TOK, HEADS * FEAT) for a in (queries, key_rows, value_rows, out_grad))
    starts = doc_starts
    swap = [(i, i ^ 1) for i in range(2 * CHIPS)]
    zgroups = [[2 * z + c for z in range(CHIPS)] for c in range(2)]
    wide = (TOK, HEADS * FEAT)
    half_states = (HALF, FEAT, FEAT)
    mm = 2 * TOK * FEAT * FEAT

    def other(x):
        return lax.ppermute(x, "seq", swap)

    def across(x):
        return lax.all_to_all(x, "seq", 0, 0, axis_index_groups=zgroups, tiled=True)

    parity = lax.rem(lax.axis_index("dp"), 2)
    row = jnp.where(
        jnp.arange(FEAT) // 64 == parity, jnp.concatenate([norm_gain, norm_gain]), 0.0
    )
    gains = lax.all_to_all(jnp.broadcast_to(row[None], (32, FEAT)), "dp", 0, 0, tiled=True)

    keep1, give1 = call(
        state_body, [(half_states, F32)] * 2, 3, 16 * mm, 2 << 20, 1 << 18
    )(starts, k, v)
    recv1 = other(give1)
    (chip,) = call(join_body, [(half_states, F32)], 3, 1 << 18, 3 << 19)(starts, keep1, recv1)
    chip, gains, after = lax.optimization_barrier((chip, gains, starts))
    parts = across(chip)
    qf, kf, scores, intra = call(
        local_body, [(wide, BF16)] * 3 + [(wide, F32)], 4, 32 * mm, 4 << 20, 1 << 19
    )(after, q, k, v)
    parts, scores = lax.optimization_barrier((parts, scores))
    (prefix,) = call(scan_body, [(half_states, F32)], 2, 1 << 18, 1 << 20)(starts, parts)
    coming = across(prefix)
    (send2,) = call(give_body, [(half_states, F32)], 3, 1 << 18, 3 << 19)(starts, keep1, coming)
    ready = other(send2)
    att, dn, inb, keep3, give3, terms = call(
        norm_body,
        [(wide, BF16), (wide, BF16), ((HEADS, FEAT, FEAT), BF16)]
        + [(half_states, F32)] * 2
        + [((32, FEAT), F32)],
        8, 32 * mm, 5 << 20, 1 << 15,
    )(starts, qf, intra, dy, gains, coming, recv1, ready)
    gathered = lax.all_to_all(terms, "dp", 0, 0, tiled=True)
    recv3 = other(give3)
    (chip3,) = call(join_back_body, [(half_states, F32)], 3, 1 << 18, 3 << 19)(starts, keep3, recv3)
    chip3, gathered, after3 = lax.optimization_barrier((chip3, gathered, starts))
    parts3 = across(chip3)
    dq, dk_part, dv_part = call(
        grads_body, [(wide, BF16), (wide, F32), (wide, F32)], 8, 80 * mm, 7 << 20, 1 << 18
    )(after3, q, v, qf, kf, scores, dn, inb)
    parts3, dk_part = lax.optimization_barrier((parts3, dk_part))
    (suffix,) = call(
        scan_back_body, [((CHIPS, FEAT + 8, FEAT), F32)], 3, 1 << 18, 1 << 20
    )(starts, parts3, gathered)
    coming4 = across(suffix)
    (send4,) = call(
        give_back_body, [((HALF * FEAT + 8, FEAT), F32)], 3, 1 << 18, 3 << 19
    )(starts, keep3, coming4)
    ready4 = other(send4)
    dk, dv, gain_grad = call(
        last_body, [(wide, BF16)] * 2 + [((1, 64), F32)], 9, 32 * mm, 5 << 20, 1 << 18
    )(starts, k, v, kf, dk_part, dv_part, recv3, coming4, ready4)
    full = (1, TOK, HEADS * FEAT)
    return (
        att.reshape(full),
        dq.reshape(full),
        dk.reshape(full),
        dv.reshape(full),
        gain_grad.reshape(64),
    )


def solution(mesh):
    rows = P("dp", "seq", None)
    return jax.shard_map(
        shards,
        mesh=mesh,
        in_specs=(rows, rows, rows, rows, P("dp"), P("dp", None)),
        out_specs=(rows, rows, rows, rows, P("dp")),
        check_vma=False,
    )
```

```python
import math

import jax
import jax.numpy as jnp
from jax import lax
from jax.experimental import pallas as pl
from jax.experimental.pallas import tpu as pltpu
from jax.sharding import PartitionSpec as P

HEADS = 16
FEAT = 128
TOK = 128
HALF = HEADS // 2
CHIPS = 8
DOCS = 8
EPS = 1e-06
F32 = jnp.float32
BF16 = jnp.bfloat16

VM = pl.BlockSpec(memory_space=pltpu.VMEM)
SM = pl.BlockSpec(memory_space=pltpu.SMEM)


def call(body, outs, n_in, flops=0, nbytes=0, trans=0, scratch=()):
    return pl.pallas_call(
        body,
        out_shape=[jax.ShapeDtypeStruct(s, d) for s, d in outs],
        in_specs=[SM] + [VM] * (n_in - 1),
        out_specs=[VM] * len(outs),
        scratch_shapes=scratch,
        compiler_params=pltpu.CompilerParams(vmem_limit_bytes=24 * 1024 * 1024),
        cost_estimate=pl.CostEstimate(
            flops=flops, bytes_accessed=nbytes, transcendentals=trans
        ),
    )


def doc_at(starts, p):
    total = jnp.int32(0)
    for j in range(DOCS):
        total = total + (starts[0, j] <= p).astype(jnp.int32)
    return total


def docs_of(starts, pos):
    total = jnp.zeros(pos.shape, jnp.int32)
    for j in range(DOCS):
        total = total + (starts[0, j] <= pos).astype(jnp.int32)
    return total


def place():
    idx = lax.axis_index("seq")
    return idx, lax.rem(idx, 2)


def row_pos(idx):
    return idx * TOK + lax.broadcasted_iota(jnp.int32, (TOK, FEAT), 0)


def enters(starts, idx):
    return docs_of(starts, row_pos(idx)) == doc_at(starts, idx * TOK - 1)


def leaves(starts, idx):
    return docs_of(starts, row_pos(idx)) == doc_at(starts, idx * TOK + TOK - 1)


def mask_of(starts, idx):
    rows = row_pos(idx)
    cols = idx * TOK + lax.broadcasted_iota(jnp.int32, (TOK, TOK), 1)
    return (rows >= cols) & (docs_of(starts, rows) == docs_of(starts, cols))


def carry_of(starts, idx):
    return (doc_at(starts, idx * TOK - 1) == doc_at(starts, idx * TOK + TOK - 1)).astype(F32)


def chip_carry(starts, z):
    first = z * 2 * TOK
    return (doc_at(starts, first - 1) == doc_at(starts, first + 2 * TOK - 1)).astype(F32)


def phi(x):
    return jnp.where(x > 0, x + 1.0, jnp.exp(jnp.minimum(x, 0.0)))


def slope(x):
    return jnp.where(x > 0, 1.0, jnp.exp(jnp.minimum(x, 0.0)))


def dot(a, b, ca, cb):
    return lax.dot_general(a, b, (((ca,), (cb,)), ((), ())), preferred_element_type=F32)


def cols(h):
    return pl.ds(pl.multiple_of(h * FEAT, FEAT), FEAT)


def state_body(starts, k, v, keep, give):
    idx, core = place()
    last = leaves(starts, idx)
    for j in range(HALF):
        for out, side in ((keep, core), (give, 1 - core)):
            at = cols(side * HALF + j)
            kf = jnp.where(last, phi(k[:, at].astype(F32)), 0.0).astype(BF16)
            out[j] = dot(kf, v[:, at], 0, 0)


def join_body(starts, keep, recv, out):
    idx, core = place()
    later = carry_of(starts, idx - core + 1)
    mine = jnp.where(core == 0, later, 1.0)
    theirs = jnp.where(core == 0, 1.0, later)
    for j in range(HALF):
        out[j] = mine * keep[j] + theirs * recv[j]


def join_back_body(starts, keep, recv, out):
    idx, core = place()
    earlier = carry_of(starts, idx - core)
    mine = jnp.where(core == 0, 1.0, earlier)
    theirs = jnp.where(core == 0, earlier, 1.0)
    for j in range(HALF):
        out[j] = mine * keep[j] + theirs * recv[j]


def scan_body(starts, parts, gain_rows, out):
    total = jnp.zeros((FEAT, FEAT), F32)
    for z in range(CHIPS):
        out[z, :FEAT] = total
        out[z, FEAT:] = gain_rows[...]
        if z < CHIPS - 1:
            total = parts[z] + chip_carry(starts, z) * total


def scan_back_body(starts, parts, terms, out):
    total = jnp.zeros((FEAT, FEAT), F32)
    gsum = jnp.broadcast_to(jnp.sum(terms[...], axis=0, keepdims=True), (8, FEAT))
    for z in reversed(range(CHIPS)):
        out[z, :FEAT] = total
        out[z, FEAT:] = gsum
        if z > 0:
            total = parts[z] + chip_carry(starts, z) * total


def give_body(starts, keep, coming, out):
    idx, core = place()
    flag = carry_of(starts, idx - core)
    a = jnp.where(core == 0, 1.0, 0.0)
    b = jnp.where(core == 0, flag, 1.0)
    for j in range(HALF):
        out[j * FEAT : (j + 1) * FEAT] = a * keep[j] + b * coming[j, :FEAT]
        out[HALF * FEAT + 8 * j : HALF * FEAT + 8 * j + 8] = coming[j, FEAT:]


def give_back_body(starts, keep, coming, out):
    idx, core = place()
    flag = carry_of(starts, idx - core + 1)
    a = jnp.where(core == 0, 0.0, 1.0)
    b = jnp.where(core == 0, 1.0, flag)
    gsum = jnp.zeros((8, FEAT), F32)
    for j in range(HALF):
        out[j * FEAT : (j + 1) * FEAT] = a * keep[j] + b * coming[j, :FEAT]
        gsum = gsum + coming[j, FEAT:]
    out[HALF * FEAT :] = gsum


def local_body(starts, q, k, v, qf_out, kf_out, scores_out, intra_out):
    idx, _ = place()
    mask = mask_of(starts, idx)
    for h in range(HEADS):
        at = slice(h * FEAT, (h + 1) * FEAT)
        qf = phi(q[:, at].astype(F32)).astype(BF16)
        kf = phi(k[:, at].astype(F32)).astype(BF16)
        qf_out[:, at] = qf
        kf_out[:, at] = kf
        scores = jnp.where(mask, dot(qf, kf, 1, 1), 0.0).astype(BF16)
        scores_out[:, at] = scores
        intra_out[:, at] = dot(scores, v[:, at], 1, 0)


def norm_body(
    starts, qf, intra, dy, coming, theirs, ready,
    att, dn_out, inb_out, keep, give, terms, gains,
):
    idx, core = place()
    y = lax.rem(lax.axis_index("dp"), CHIPS)
    for j in range(CHIPS):
        at = HALF * FEAT + 8 * j
        gains[8 * j : 8 * j + 8, :] = coming[j, FEAT:] + ready[at : at + 8]
    cin = enters(starts, idx)
    flag = carry_of(starts, idx - core)
    a = jnp.where(core == 0, 0.0, 1.0)
    b = jnp.where(core == 0, 1.0, flag)
    for j in range(HALF):
        for side, state in ((core, keep), (1 - core, give)):
            h = side * HALF + j
            at = cols(h)
            if state is keep:
                incoming = a * theirs[j] + b * coming[j, :FEAT]
            else:
                incoming = ready[j * FEAT : (j + 1) * FEAT]
            inb = incoming.astype(BF16)
            inb_out[h] = inb
            qh = qf[:, at]
            num = intra[:, at] + jnp.where(cin, dot(qh, inb, 1, 0), 0.0)
            recip = lax.rsqrt(jnp.mean(num * num, -1, keepdims=True) + EPS)
            normed = num * recip
            even = lax.rem(2 * lax.rem(h, 4) - y + CHIPS, CHIPS)
            odd = lax.rem(2 * lax.rem(h, 4) + 1 - y + CHIPS, CHIPS)
            gain = gains[pl.ds(8 * even + h // 4, 1), :] + gains[pl.ds(8 * odd + h // 4, 1), :]
            att[:, at] = (normed * gain).astype(BF16)
            grad = dy[:, at].astype(F32)
            upper = grad * gain
            mean = jnp.mean(upper * normed, -1, keepdims=True)
            dn = (recip * upper - normed * recip * mean).astype(BF16)
            dn_out[:, at] = dn
            term = jnp.sum(grad * normed, axis=0, keepdims=True)
            terms[pl.ds(2 * h, 1), :] = term
            terms[pl.ds(2 * h + 1, 1), :] = term
            masked = jnp.where(cin, dn, jnp.zeros_like(dn))
            state[j] = dot(qh, masked, 0, 0)


def grads_body(starts, q, v, qf, kf, scores, dn, inb, dq_out, dk_part, dv_part):
    idx, _ = place()
    mask = mask_of(starts, idx)
    cin = enters(starts, idx)
    for h in range(HEADS):
        at = slice(h * FEAT, (h + 1) * FEAT)
        dnh = dn[:, at]
        dscores = jnp.where(mask, dot(dnh, v[:, at], 1, 1), 0.0).astype(BF16)
        dq = dot(dscores, kf[:, at], 1, 0) + jnp.where(cin, dot(dnh, inb[h], 1, 1), 0.0)
        dq_out[:, at] = (dq * slope(q[:, at].astype(F32))).astype(BF16)
        dk_part[:, at] = dot(dscores, qf[:, at], 0, 0)
        dv_part[:, at] = dot(scores[:, at], dnh, 0, 0)


def last_body(
    starts, k, v, kf, dk_part, dv_part, theirs, coming, ready,
    dk_out, dv_out, gain_out,
):
    idx, core = place()
    last = leaves(starts, idx)
    flag = carry_of(starts, idx - core + 1)
    a = jnp.where(core == 0, 1.0, 0.0)
    b = jnp.where(core == 0, flag, 1.0)
    gsum = ready[HALF * FEAT :]
    for j in range(HALF):
        gsum = gsum + coming[j, FEAT:]
        for mine, side in ((True, core), (False, 1 - core)):
            at = cols(side * HALF + j)
            if mine:
                outgoing = a * theirs[j] + b * coming[j, :FEAT]
            else:
                outgoing = ready[j * FEAT : (j + 1) * FEAT]
            outb = outgoing.astype(BF16)
            dk = dk_part[:, at] + jnp.where(last, dot(v[:, at], outb, 1, 1), 0.0)
            dk_out[:, at] = (dk * slope(k[:, at].astype(F32))).astype(BF16)
            dv = dv_part[:, at] + jnp.where(last, dot(kf[:, at], outb, 1, 0), 0.0)
            dv_out[:, at] = dv.astype(BF16)
    half = lax.rem(lax.axis_index("dp"), 2)
    total = gsum[:1] * (1.0 / math.sqrt(32 * 2048))
    gain_out[...] = jnp.where(half == 0, total[:, :64], total[:, 64:])


def shards(queries, key_rows, value_rows, out_grad, norm_gain, doc_starts):
    q, k, v, dy = (a.reshape(TOK, HEADS * FEAT) for a in (queries, key_rows, value_rows, out_grad))
    starts = doc_starts
    swap = [(i, i ^ 1) for i in range(2 * CHIPS)]
    zgroups = [[2 * z + c for z in range(CHIPS)] for c in range(2)]
    wide = (TOK, HEADS * FEAT)
    half_states = (HALF, FEAT, FEAT)
    mm = 2 * TOK * FEAT * FEAT

    def other(x):
        return lax.ppermute(x, "seq", swap)

    def across(x):
        return lax.all_to_all(x, "seq", 0, 0, axis_index_groups=zgroups, tiled=True)

    part = lax.axis_index("dp")
    row = jnp.where(
        (jnp.arange(8)[:, None] == part // CHIPS) & (jnp.arange(FEAT)[None] // 64 == part % 2),
        jnp.concatenate([norm_gain, norm_gain])[None],
        0.0,
    )
    row = row + lax.ppermute(row, "dp", [(i, i ^ CHIPS) for i in range(4 * CHIPS)])
    shifted = [
        ((((x ^ (2 * c)) * CHIPS + (y + z) % CHIPS) * CHIPS + z) * 2 + c, ((x * CHIPS + y) * CHIPS + z) * 2 + c)
        for x in range(4) for y in range(CHIPS) for z in range(CHIPS) for c in range(2)
    ]
    gain_rows = lax.ppermute(row, ("dp", "seq"), shifted)

    keep1, give1 = call(
        state_body, [(half_states, F32)] * 2, 3, 16 * mm, 2 << 20, 1 << 18
    )(starts, k, v)
    recv1 = other(give1)
    (chip,) = call(join_body, [(half_states, F32)], 3, 1 << 18, 3 << 19)(starts, keep1, recv1)
    parts = across(chip)
    (prefix,) = call(
        scan_body, [((CHIPS, FEAT + 8, FEAT), F32)], 3, 1 << 18, 1 << 20
    )(starts, parts, gain_rows)
    prefix, after = lax.optimization_barrier((prefix, starts))
    coming = across(prefix)
    qf, kf, scores, intra = call(
        local_body, [(wide, BF16)] * 3 + [(wide, F32)], 4, 32 * mm, 4 << 20, 1 << 19
    )(after, q, k, v)
    coming, scores = lax.optimization_barrier((coming, scores))
    (send2,) = call(
        give_body, [((HALF * FEAT + 64, FEAT), F32)], 3, 1 << 18, 3 << 19
    )(starts, keep1, coming)
    ready = other(send2)
    att, dn, inb, keep3, give3, terms = call(
        norm_body,
        [(wide, BF16), (wide, BF16), ((HEADS, FEAT, FEAT), BF16)]
        + [(half_states, F32)] * 2
        + [((32, FEAT), F32)],
        7, 32 * mm, 5 << 20, 1 << 15, scratch=[pltpu.VMEM((64, FEAT), F32)],
    )(starts, qf, intra, dy, coming, recv1, ready)
    gathered = lax.all_to_all(terms, "dp", 0, 0, tiled=True)
    recv3 = other(give3)
    (chip3,) = call(join_back_body, [(half_states, F32)], 3, 1 << 18, 3 << 19)(starts, keep3, recv3)
    chip3, gathered, after3 = lax.optimization_barrier((chip3, gathered, starts))
    parts3 = across(chip3)
    dq, dk_part, dv_part = call(
        grads_body, [(wide, BF16), (wide, F32), (wide, F32)], 8, 80 * mm, 7 << 20, 1 << 18
    )(after3, q, v, qf, kf, scores, dn, inb)
    parts3, dk_part = lax.optimization_barrier((parts3, dk_part))
    (suffix,) = call(
        scan_back_body, [((CHIPS, FEAT + 8, FEAT), F32)], 3, 1 << 18, 1 << 20
    )(starts, parts3, gathered)
    coming4 = across(suffix)
    (send4,) = call(
        give_back_body, [((HALF * FEAT + 8, FEAT), F32)], 3, 1 << 18, 3 << 19
    )(starts, keep3, coming4)
    ready4 = other(send4)
    dk, dv, gain_grad = call(
        last_body, [(wide, BF16)] * 2 + [((1, 64), F32)], 9, 32 * mm, 5 << 20, 1 << 18
    )(starts, k, v, kf, dk_part, dv_part, recv3, coming4, ready4)
    full = (1, TOK, HEADS * FEAT)
    return (
        att.reshape(full),
        dq.reshape(full),
        dk.reshape(full),
        dv.reshape(full),
        gain_grad.reshape(64),
    )


def solution(mesh):
    rows = P("dp", "seq", None)
    return jax.shard_map(
        shards,
        mesh=mesh,
        in_specs=(rows, rows, rows, rows, P("dp"), P("dp", None)),
        out_specs=(rows, rows, rows, rows, P("dp")),
        check_vma=False,
    )
```

```python
import math

import jax
import jax.numpy as jnp
from jax import lax
from jax.experimental import pallas as pl
from jax.experimental.pallas import tpu as pltpu
from jax.sharding import PartitionSpec as P

HEADS = 16
FEAT = 128
TOK = 128
HALF = HEADS // 2
CHIPS = 8
DOCS = 8
EPS = 1e-06
F32 = jnp.float32
BF16 = jnp.bfloat16

VM = pl.BlockSpec(memory_space=pltpu.VMEM)
SM = pl.BlockSpec(memory_space=pltpu.SMEM)
HB = pl.BlockSpec(memory_space=pltpu.HBM)


def call(body, outs, n_in, flops=0, nbytes=0, trans=0, far=False, scratch=()):
    return pl.pallas_call(
        body,
        out_shape=[pltpu.HBM(s, d) if far else jax.ShapeDtypeStruct(s, d) for s, d in outs],
        in_specs=[SM] + [VM] * (n_in - 1),
        out_specs=[HB if far else VM] * len(outs),
        scratch_shapes=scratch,
        compiler_params=pltpu.CompilerParams(vmem_limit_bytes=24 * 1024 * 1024),
        cost_estimate=pl.CostEstimate(
            flops=flops, bytes_accessed=nbytes, transcendentals=trans
        ),
    )


def doc_at(starts, p):
    total = jnp.int32(0)
    for j in range(DOCS):
        total = total + (starts[0, j] <= p).astype(jnp.int32)
    return total


def docs_of(starts, pos):
    total = jnp.zeros(pos.shape, jnp.int32)
    for j in range(DOCS):
        total = total + (starts[0, j] <= pos).astype(jnp.int32)
    return total


def place():
    idx = lax.axis_index("seq")
    return idx, lax.rem(idx, 2)


def row_pos(idx):
    return idx * TOK + lax.broadcasted_iota(jnp.int32, (TOK, FEAT), 0)


def enters(starts, idx):
    return docs_of(starts, row_pos(idx)) == doc_at(starts, idx * TOK - 1)


def leaves(starts, idx):
    return docs_of(starts, row_pos(idx)) == doc_at(starts, idx * TOK + TOK - 1)


def mask_of(starts, idx):
    rows = row_pos(idx)
    cols = idx * TOK + lax.broadcasted_iota(jnp.int32, (TOK, TOK), 1)
    return (rows >= cols) & (docs_of(starts, rows) == docs_of(starts, cols))


def carry_of(starts, idx):
    return (doc_at(starts, idx * TOK - 1) == doc_at(starts, idx * TOK + TOK - 1)).astype(F32)


def chip_carry(starts, z):
    first = z * 2 * TOK
    return (doc_at(starts, first - 1) == doc_at(starts, first + 2 * TOK - 1)).astype(F32)


def phi(x):
    return jnp.where(x > 0, x + 1.0, jnp.exp(jnp.minimum(x, 0.0)))


def slope(x):
    return jnp.where(x > 0, 1.0, jnp.exp(jnp.minimum(x, 0.0)))


def dot(a, b, ca, cb):
    return lax.dot_general(a, b, (((ca,), (cb,)), ((), ())), preferred_element_type=F32)


def cols(h):
    return pl.ds(pl.multiple_of(h * FEAT, FEAT), FEAT)


def state_body(starts, k, v, keep, give):
    idx, core = place()
    last = leaves(starts, idx)
    for j in range(HALF):
        for out, side in ((keep, core), (give, 1 - core)):
            at = cols(side * HALF + j)
            kf = jnp.where(last, phi(k[:, at].astype(F32)), 0.0).astype(BF16)
            out[j] = dot(kf, v[:, at], 0, 0)


def join_body(starts, keep, recv, out):
    idx, core = place()
    later = carry_of(starts, idx - core + 1)
    mine = jnp.where(core == 0, later, 1.0)
    theirs = jnp.where(core == 0, 1.0, later)
    for j in range(HALF):
        out[j] = mine * keep[j] + theirs * recv[j]


def join_back_body(starts, keep, recv, out):
    idx, core = place()
    earlier = carry_of(starts, idx - core)
    mine = jnp.where(core == 0, 1.0, earlier)
    theirs = jnp.where(core == 0, earlier, 1.0)
    for j in range(HALF):
        out[j] = mine * keep[j] + theirs * recv[j]


def scan_body(starts, parts, gain_rows, out):
    total = jnp.zeros((FEAT, FEAT), F32)
    for z in range(CHIPS):
        out[z, :FEAT] = total
        out[z, FEAT:] = gain_rows[...]
        if z < CHIPS - 1:
            total = parts[z] + chip_carry(starts, z) * total


def scan_back_body(starts, parts, terms, out):
    total = jnp.zeros((FEAT, FEAT), F32)
    gsum = jnp.broadcast_to(jnp.sum(terms[...], axis=0, keepdims=True), (8, FEAT))
    for z in reversed(range(CHIPS)):
        out[z, :FEAT] = total
        out[z, FEAT:] = gsum
        if z > 0:
            total = parts[z] + chip_carry(starts, z) * total


def give_body(starts, keep, coming, out):
    idx, core = place()
    flag = carry_of(starts, idx - core)
    a = jnp.where(core == 0, 1.0, 0.0)
    b = jnp.where(core == 0, flag, 1.0)
    for j in range(HALF):
        out[j * FEAT : (j + 1) * FEAT] = a * keep[j] + b * coming[j, :FEAT]
        out[HALF * FEAT + 8 * j : HALF * FEAT + 8 * j + 8] = coming[j, FEAT:]


def give_back_body(starts, keep, coming, out):
    idx, core = place()
    flag = carry_of(starts, idx - core + 1)
    a = jnp.where(core == 0, 0.0, 1.0)
    b = jnp.where(core == 0, 1.0, flag)
    gsum = jnp.zeros((8, FEAT), F32)
    for j in range(HALF):
        out[j * FEAT : (j + 1) * FEAT] = a * keep[j] + b * coming[j, :FEAT]
        gsum = gsum + coming[j, FEAT:]
    out[HALF * FEAT :] = gsum


def local_body(
    starts, q, k, v, qf_out, kf_out, scores_out, intra_out,
    qf_buf, kf_buf, scores_buf, intra_buf, sems,
):
    idx, _ = place()
    mask = mask_of(starts, idx)
    pairs = (
        (qf_buf, qf_out), (kf_buf, kf_out), (scores_buf, scores_out), (intra_buf, intra_out),
    )
    copies = []
    for h in range(HEADS):
        at = slice(h * FEAT, (h + 1) * FEAT)
        qf = phi(q[:, at].astype(F32)).astype(BF16)
        kf = phi(k[:, at].astype(F32)).astype(BF16)
        qf_buf[:, at] = qf
        kf_buf[:, at] = kf
        scores = jnp.where(mask, dot(qf, kf, 1, 1), 0.0).astype(BF16)
        scores_buf[:, at] = scores
        intra_buf[:, at] = dot(scores, v[:, at], 1, 0)
        if h % 4 == 3:
            group = pl.ds((h - 3) * FEAT, 4 * FEAT)
            for n, (buf, out) in enumerate(pairs):
                c = pltpu.make_async_copy(buf.at[:, group], out.at[:, group], sems.at[h - 3 + n])
                c.start()
                copies.append(c)
    for c in copies:
        c.wait()


def norm_body(
    starts, qf, intra, dy, coming, theirs, ready,
    att, dn_out, inb_out, keep, give, terms, gains,
):
    idx, core = place()
    y = lax.rem(lax.axis_index("dp"), CHIPS)
    for j in range(CHIPS):
        at = HALF * FEAT + 8 * j
        gains[8 * j : 8 * j + 8, :] = coming[j, FEAT:] + ready[at : at + 8]
    cin = enters(starts, idx)
    flag = carry_of(starts, idx - core)
    a = jnp.where(core == 0, 0.0, 1.0)
    b = jnp.where(core == 0, 1.0, flag)
    for j in range(HALF):
        for side, state in ((core, keep), (1 - core, give)):
            h = side * HALF + j
            at = cols(h)
            if state is keep:
                incoming = a * theirs[j] + b * coming[j, :FEAT]
            else:
                incoming = ready[j * FEAT : (j + 1) * FEAT]
            inb = incoming.astype(BF16)
            inb_out[h] = inb
            qh = qf[:, at]
            num = intra[:, at] + jnp.where(cin, dot(qh, inb, 1, 0), 0.0)
            recip = lax.rsqrt(jnp.mean(num * num, -1, keepdims=True) + EPS)
            normed = num * recip
            even = lax.rem(2 * lax.rem(h, 4) - y + CHIPS, CHIPS)
            odd = lax.rem(2 * lax.rem(h, 4) + 1 - y + CHIPS, CHIPS)
            gain = gains[pl.ds(8 * even + h // 4, 1), :] + gains[pl.ds(8 * odd + h // 4, 1), :]
            att[:, at] = (normed * gain).astype(BF16)
            grad = dy[:, at].astype(F32)
            upper = grad * gain
            mean = jnp.mean(upper * normed, -1, keepdims=True)
            dn = (recip * upper - normed * recip * mean).astype(BF16)
            dn_out[:, at] = dn
            term = jnp.sum(grad * normed, axis=0, keepdims=True)
            terms[pl.ds(2 * h, 1), :] = term
            terms[pl.ds(2 * h + 1, 1), :] = term
            masked = jnp.where(cin, dn, jnp.zeros_like(dn))
            state[j] = dot(qh, masked, 0, 0)


def grads_body(starts, q, v, qf, kf, scores, dn, inb, dq_out, dk_part, dv_part):
    idx, _ = place()
    mask = mask_of(starts, idx)
    cin = enters(starts, idx)
    for h in range(HEADS):
        at = slice(h * FEAT, (h + 1) * FEAT)
        dnh = dn[:, at]
        dscores = jnp.where(mask, dot(dnh, v[:, at], 1, 1), 0.0).astype(BF16)
        dq = dot(dscores, kf[:, at], 1, 0) + jnp.where(cin, dot(dnh, inb[h], 1, 1), 0.0)
        dq_out[:, at] = (dq * slope(q[:, at].astype(F32))).astype(BF16)
        dk_part[:, at] = dot(dscores, qf[:, at], 0, 0)
        dv_part[:, at] = dot(scores[:, at], dnh, 0, 0)


def last_body(
    starts, k, v, kf, dk_part, dv_part, theirs, coming, ready,
    dk_out, dv_out, gain_out,
):
    idx, core = place()
    last = leaves(starts, idx)
    flag = carry_of(starts, idx - core + 1)
    a = jnp.where(core == 0, 1.0, 0.0)
    b = jnp.where(core == 0, flag, 1.0)
    gsum = ready[HALF * FEAT :]
    for j in range(HALF):
        gsum = gsum + coming[j, FEAT:]
        for mine, side in ((True, core), (False, 1 - core)):
            at = cols(side * HALF + j)
            if mine:
                outgoing = a * theirs[j] + b * coming[j, :FEAT]
            else:
                outgoing = ready[j * FEAT : (j + 1) * FEAT]
            outb = outgoing.astype(BF16)
            dk = dk_part[:, at] + jnp.where(last, dot(v[:, at], outb, 1, 1), 0.0)
            dk_out[:, at] = (dk * slope(k[:, at].astype(F32))).astype(BF16)
            dv = dv_part[:, at] + jnp.where(last, dot(kf[:, at], outb, 1, 0), 0.0)
            dv_out[:, at] = dv.astype(BF16)
    half = lax.rem(lax.axis_index("dp"), 2)
    total = gsum[:1] * (1.0 / math.sqrt(32 * 2048))
    gain_out[...] = jnp.where(half == 0, total[:, :64], total[:, 64:])


def shards(queries, key_rows, value_rows, out_grad, norm_gain, doc_starts):
    q, k, v, dy = (a.reshape(TOK, HEADS * FEAT) for a in (queries, key_rows, value_rows, out_grad))
    starts = doc_starts
    swap = [(i, i ^ 1) for i in range(2 * CHIPS)]
    zgroups = [[2 * z + c for z in range(CHIPS)] for c in range(2)]
    wide = (TOK, HEADS * FEAT)
    half_states = (HALF, FEAT, FEAT)
    mm = 2 * TOK * FEAT * FEAT

    def other(x):
        return lax.ppermute(x, "seq", swap)

    def across(x):
        return lax.all_to_all(x, "seq", 0, 0, axis_index_groups=zgroups, tiled=True)

    part = lax.axis_index("dp")
    row = jnp.where(
        (jnp.arange(8)[:, None] == part // CHIPS) & (jnp.arange(FEAT)[None] // 64 == part % 2),
        jnp.concatenate([norm_gain, norm_gain])[None],
        0.0,
    )
    row = row + lax.ppermute(row, "dp", [(i, i ^ CHIPS) for i in range(4 * CHIPS)])
    keep1, give1 = call(
        state_body, [(half_states, F32)] * 2, 3, 16 * mm, 2 << 20, 1 << 18
    )(starts, k, v)
    recv1 = other(give1)
    (chip,) = call(join_body, [(half_states, F32)], 3, 1 << 18, 3 << 19)(starts, keep1, recv1)
    chip, row, after = lax.optimization_barrier((chip, row, starts))
    parts = across(chip)
    shifted = [
        ((((x ^ (2 * c)) * CHIPS + (y + z) % CHIPS) * CHIPS + z) * 2 + c, ((x * CHIPS + y) * CHIPS + z) * 2 + c)
        for x in range(4) for y in range(CHIPS) for z in range(CHIPS) for c in range(2)
    ]
    gain_rows = lax.ppermute(row, ("dp", "seq"), shifted)
    qf, kf, scores, intra = call(
        local_body, [(wide, BF16)] * 3 + [(wide, F32)], 4, 32 * mm, 4 << 20, 1 << 19, far=True,
        scratch=[pltpu.VMEM(wide, BF16)] * 3 + [pltpu.VMEM(wide, F32), pltpu.SemaphoreType.DMA((16,))],
    )(after, q, k, v)
    parts, scores = lax.optimization_barrier((parts, scores))
    (prefix,) = call(
        scan_body, [((CHIPS, FEAT + 8, FEAT), F32)], 3, 1 << 18, 1 << 20
    )(starts, parts, gain_rows)
    coming = across(prefix)
    (send2,) = call(
        give_body, [((HALF * FEAT + 64, FEAT), F32)], 3, 1 << 18, 3 << 19
    )(starts, keep1, coming)
    ready = other(send2)
    att, dn, inb, keep3, give3, terms = call(
        norm_body,
        [(wide, BF16), (wide, BF16), ((HEADS, FEAT, FEAT), BF16)]
        + [(half_states, F32)] * 2
        + [((32, FEAT), F32)],
        7, 32 * mm, 5 << 20, 1 << 15, scratch=[pltpu.VMEM((64, FEAT), F32)],
    )(starts, qf, intra, dy, coming, recv1, ready)
    gathered = lax.all_to_all(terms, "dp", 0, 0, tiled=True)
    recv3 = other(give3)
    (chip3,) = call(join_back_body, [(half_states, F32)], 3, 1 << 18, 3 << 19)(starts, keep3, recv3)
    chip3, gathered, after3 = lax.optimization_barrier((chip3, gathered, starts))
    parts3 = across(chip3)
    dq, dk_part, dv_part = call(
        grads_body, [(wide, BF16), (wide, F32), (wide, F32)], 8, 80 * mm, 7 << 20, 1 << 18
    )(after3, q, v, qf, kf, scores, dn, inb)
    parts3, dk_part = lax.optimization_barrier((parts3, dk_part))
    (suffix,) = call(
        scan_back_body, [((CHIPS, FEAT + 8, FEAT), F32)], 3, 1 << 18, 1 << 20
    )(starts, parts3, gathered)
    coming4 = across(suffix)
    (send4,) = call(
        give_back_body, [((HALF * FEAT + 8, FEAT), F32)], 3, 1 << 18, 3 << 19
    )(starts, keep3, coming4)
    ready4 = other(send4)
    dk, dv, gain_grad = call(
        last_body, [(wide, BF16)] * 2 + [((1, 64), F32)], 9, 32 * mm, 5 << 20, 1 << 18
    )(starts, k, v, kf, dk_part, dv_part, recv3, coming4, ready4)
    full = (1, TOK, HEADS * FEAT)
    return (
        att.reshape(full),
        dq.reshape(full),
        dk.reshape(full),
        dv.reshape(full),
        gain_grad.reshape(64),
    )


def solution(mesh):
    rows = P("dp", "seq", None)
    return jax.shard_map(
        shards,
        mesh=mesh,
        in_specs=(rows, rows, rows, rows, P("dp"), P("dp", None)),
        out_specs=(rows, rows, rows, rows, P("dp")),
        check_vma=False,
    )
```

```python
import math

import jax
import jax.numpy as jnp
from jax import lax
from jax.experimental import pallas as pl
from jax.experimental.pallas import tpu as pltpu
from jax.sharding import PartitionSpec as P

HEADS = 16
FEAT = 128
TOK = 128
HALF = HEADS // 2
CHIPS = 8
DOCS = 8
EPS = 1e-06
F32 = jnp.float32
BF16 = jnp.bfloat16

VM = pl.BlockSpec(memory_space=pltpu.VMEM)
SM = pl.BlockSpec(memory_space=pltpu.SMEM)
HB = pl.BlockSpec(memory_space=pltpu.HBM)


def call(body, outs, n_in, flops=0, nbytes=0, trans=0, far=False, far_in=(), scratch=()):
    return pl.pallas_call(
        body,
        out_shape=[pltpu.HBM(s, d) if far else jax.ShapeDtypeStruct(s, d) for s, d in outs],
        in_specs=[SM] + [HB if i in far_in else VM for i in range(1, n_in)],
        out_specs=[HB if far else VM] * len(outs),
        scratch_shapes=scratch,
        compiler_params=pltpu.CompilerParams(vmem_limit_bytes=24 * 1024 * 1024),
        cost_estimate=pl.CostEstimate(
            flops=flops, bytes_accessed=nbytes, transcendentals=trans
        ),
    )


def doc_at(starts, p):
    total = jnp.int32(0)
    for j in range(DOCS):
        total = total + (starts[0, j] <= p).astype(jnp.int32)
    return total


def docs_of(starts, pos):
    total = jnp.zeros(pos.shape, jnp.int32)
    for j in range(DOCS):
        total = total + (starts[0, j] <= pos).astype(jnp.int32)
    return total


def place():
    idx = lax.axis_index("seq")
    return idx, lax.rem(idx, 2)


def row_pos(idx):
    return idx * TOK + lax.broadcasted_iota(jnp.int32, (TOK, FEAT), 0)


def enters(starts, idx):
    return docs_of(starts, row_pos(idx)) == doc_at(starts, idx * TOK - 1)


def leaves(starts, idx):
    return docs_of(starts, row_pos(idx)) == doc_at(starts, idx * TOK + TOK - 1)


def mask_of(starts, idx):
    rows = row_pos(idx)
    cols = idx * TOK + lax.broadcasted_iota(jnp.int32, (TOK, TOK), 1)
    return (rows >= cols) & (docs_of(starts, rows) == docs_of(starts, cols))


def carry_of(starts, idx):
    return (doc_at(starts, idx * TOK - 1) == doc_at(starts, idx * TOK + TOK - 1)).astype(F32)


def chip_carry(starts, z):
    first = z * 2 * TOK
    return (doc_at(starts, first - 1) == doc_at(starts, first + 2 * TOK - 1)).astype(F32)


def phi(x):
    return jnp.where(x > 0, x + 1.0, jnp.exp(jnp.minimum(x, 0.0)))


def slope(x):
    return jnp.where(x > 0, 1.0, jnp.exp(jnp.minimum(x, 0.0)))


def dot(a, b, ca, cb):
    return lax.dot_general(a, b, (((ca,), (cb,)), ((), ())), preferred_element_type=F32)


def cols(h):
    return pl.ds(pl.multiple_of(h * FEAT, FEAT), FEAT)


def state_body(starts, k, v, keep, give):
    idx, core = place()
    last = leaves(starts, idx)
    for j in range(HALF):
        for out, side in ((keep, core), (give, 1 - core)):
            at = cols(side * HALF + j)
            kf = jnp.where(last, phi(k[:, at].astype(F32)), 0.0).astype(BF16)
            out[j] = dot(kf, v[:, at], 0, 0)


def join_body(starts, keep, recv, out):
    idx, core = place()
    later = carry_of(starts, idx - core + 1)
    mine = jnp.where(core == 0, later, 1.0)
    theirs = jnp.where(core == 0, 1.0, later)
    for j in range(HALF):
        out[j] = mine * keep[j] + theirs * recv[j]


def join_back_body(starts, keep, recv, out):
    idx, core = place()
    earlier = carry_of(starts, idx - core)
    mine = jnp.where(core == 0, 1.0, earlier)
    theirs = jnp.where(core == 0, earlier, 1.0)
    for j in range(HALF):
        out[j] = mine * keep[j] + theirs * recv[j]


def scan_body(starts, parts, gain_rows, out):
    total = jnp.zeros((FEAT, FEAT), F32)
    for z in range(CHIPS):
        out[z, :FEAT] = total
        out[z, FEAT:] = gain_rows[...]
        if z < CHIPS - 1:
            total = parts[z] + chip_carry(starts, z) * total


def scan_back_body(starts, parts, terms, out):
    total = jnp.zeros((FEAT, FEAT), F32)
    x = lax.axis_index("dp") // CHIPS
    gsum = jnp.broadcast_to(terms[pl.ds(x, 1), :], (8, FEAT))
    for z in reversed(range(CHIPS)):
        out[z, :FEAT] = total
        out[z, FEAT:] = gsum
        if z > 0:
            total = parts[z] + chip_carry(starts, z) * total


def give_body(starts, keep, coming, out):
    idx, core = place()
    flag = carry_of(starts, idx - core)
    a = jnp.where(core == 0, 1.0, 0.0)
    b = jnp.where(core == 0, flag, 1.0)
    for j in range(HALF):
        out[j * FEAT : (j + 1) * FEAT] = a * keep[j] + b * coming[j, :FEAT]
        out[HALF * FEAT + 8 * j : HALF * FEAT + 8 * j + 8] = coming[j, FEAT:]


def give_back_body(starts, keep, coming, out):
    idx, core = place()
    flag = carry_of(starts, idx - core + 1)
    a = jnp.where(core == 0, 0.0, 1.0)
    b = jnp.where(core == 0, 1.0, flag)
    gsum = jnp.zeros((8, FEAT), F32)
    for j in range(HALF):
        out[j * FEAT : (j + 1) * FEAT] = a * keep[j] + b * coming[j, :FEAT]
        gsum = gsum + coming[j, FEAT:]
    out[HALF * FEAT :] = gsum


def local_body(
    starts, q, k, v, qf_out, kf_out, scores_out, intra_out,
    qf_buf, kf_buf, scores_buf, intra_buf, sems,
):
    idx, _ = place()
    mask = mask_of(starts, idx)
    pairs = (
        (qf_buf, qf_out), (kf_buf, kf_out), (scores_buf, scores_out), (intra_buf, intra_out),
    )
    copies = []
    for h in range(HEADS):
        at = slice(h * FEAT, (h + 1) * FEAT)
        qf = phi(q[:, at].astype(F32)).astype(BF16)
        kf = phi(k[:, at].astype(F32)).astype(BF16)
        qf_buf[:, at] = qf
        kf_buf[:, at] = kf
        scores = jnp.where(mask, dot(qf, kf, 1, 1), 0.0).astype(BF16)
        scores_buf[:, at] = scores
        intra_buf[:, at] = dot(scores, v[:, at], 1, 0)
        if h % 4 == 3:
            group = pl.ds((h - 3) * FEAT, 4 * FEAT)
            for n, (buf, out) in enumerate(pairs):
                c = pltpu.make_async_copy(buf.at[:, group], out.at[:, group], sems.at[h - 3 + n])
                c.start()
                copies.append(c)
    for c in copies:
        c.wait()


def norm_body(
    starts, qf, intra, dy, coming, theirs, ready,
    att, dn_out, inb_out, keep, give, terms, gains,
):
    idx, core = place()
    y = lax.rem(lax.axis_index("dp"), CHIPS)
    terms[...] = jnp.zeros_like(terms)
    for j in range(CHIPS):
        at = HALF * FEAT + 8 * j
        gains[8 * j : 8 * j + 8, :] = coming[j, FEAT:] + ready[at : at + 8]
    cin = enters(starts, idx)
    flag = carry_of(starts, idx - core)
    a = jnp.where(core == 0, 0.0, 1.0)
    b = jnp.where(core == 0, 1.0, flag)
    for j in range(HALF):
        for side, state in ((core, keep), (1 - core, give)):
            h = side * HALF + j
            at = cols(h)
            if state is keep:
                incoming = a * theirs[j] + b * coming[j, :FEAT]
            else:
                incoming = ready[j * FEAT : (j + 1) * FEAT]
            inb = incoming.astype(BF16)
            inb_out[h] = inb
            qh = qf[:, at]
            num = intra[:, at] + jnp.where(cin, dot(qh, inb, 1, 0), 0.0)
            recip = lax.rsqrt(jnp.mean(num * num, -1, keepdims=True) + EPS)
            normed = num * recip
            even = lax.rem(2 * lax.rem(h, 4) - y + CHIPS, CHIPS)
            odd = lax.rem(2 * lax.rem(h, 4) + 1 - y + CHIPS, CHIPS)
            gain = gains[pl.ds(8 * even + h // 4, 1), :] + gains[pl.ds(8 * odd + h // 4, 1), :]
            att[:, at] = (normed * gain).astype(BF16)
            grad = dy[:, at].astype(F32)
            upper = grad * gain
            mean = jnp.mean(upper * normed, -1, keepdims=True)
            dn = (recip * upper - normed * recip * mean).astype(BF16)
            dn_out[:, at] = dn
            term = jnp.sum(grad * normed, axis=0, keepdims=True)
            to = 16 * lax.rem(h, 4) + h // 4
            terms[pl.ds(to, 1), :] = term
            terms[pl.ds(to + 8, 1), :] = term
            masked = jnp.where(cin, dn, jnp.zeros_like(dn))
            state[j] = dot(qh, masked, 0, 0)


def grads_body(starts, *refs):
    ins, outs, in_bufs, out_bufs, sems = refs[:7], refs[7:10], refs[10:17], refs[17:20], refs[20]
    q, v, qf, kf, scores, dn, inb = in_bufs
    dq_buf, dk_buf, dv_buf = out_bufs
    groups = [pl.ds(4 * g * FEAT, 4 * FEAT) for g in range(4)]
    coming, going = [], []
    for g in range(4):
        these = []
        for n in range(7):
            if n < 6:
                src, dst = ins[n].at[:, groups[g]], in_bufs[n].at[:, groups[g]]
            else:
                src, dst = ins[n].at[pl.ds(4 * g, 4)], in_bufs[n].at[pl.ds(4 * g, 4)]
            these.append(pltpu.make_async_copy(src, dst, sems.at[10 * g + n]))
        for c in these:
            c.start()
        coming.append(these)
    idx, _ = place()
    mask = mask_of(starts, idx)
    cin = enters(starts, idx)
    for h in range(HEADS):
        g = h // 4
        if h % 4 == 0:
            for c in coming[g]:
                c.wait()
        at = slice(h * FEAT, (h + 1) * FEAT)
        dnh = dn[:, at]
        dscores = jnp.where(mask, dot(dnh, v[:, at], 1, 1), 0.0).astype(BF16)
        dq = dot(dscores, kf[:, at], 1, 0) + jnp.where(cin, dot(dnh, inb[h], 1, 1), 0.0)
        dq_buf[:, at] = (dq * slope(q[:, at].astype(F32))).astype(BF16)
        dk_buf[:, at] = dot(dscores, qf[:, at], 0, 0)
        dv_buf[:, at] = dot(scores[:, at], dnh, 0, 0)
        if h % 4 == 3:
            for n in range(3):
                c = pltpu.make_async_copy(
                    out_bufs[n].at[:, groups[g]], outs[n].at[:, groups[g]], sems.at[10 * g + 7 + n]
                )
                c.start()
                going.append(c)
    for c in going:
        c.wait()


def last_body(
    starts, k, v, kf, dk_part, dv_part, theirs, coming, ready,
    dk_out, dv_out, gain_out,
):
    idx, core = place()
    last = leaves(starts, idx)
    flag = carry_of(starts, idx - core + 1)
    a = jnp.where(core == 0, 1.0, 0.0)
    b = jnp.where(core == 0, flag, 1.0)
    gsum = ready[HALF * FEAT :]
    for j in range(HALF):
        gsum = gsum + coming[j, FEAT:]
        for mine, side in ((True, core), (False, 1 - core)):
            at = cols(side * HALF + j)
            if mine:
                outgoing = a * theirs[j] + b * coming[j, :FEAT]
            else:
                outgoing = ready[j * FEAT : (j + 1) * FEAT]
            outb = outgoing.astype(BF16)
            dk = dk_part[:, at] + jnp.where(last, dot(v[:, at], outb, 1, 1), 0.0)
            dk_out[:, at] = (dk * slope(k[:, at].astype(F32))).astype(BF16)
            dv = dv_part[:, at] + jnp.where(last, dot(kf[:, at], outb, 1, 0), 0.0)
            dv_out[:, at] = dv.astype(BF16)
    half = lax.rem(lax.axis_index("dp"), 2)
    total = gsum[:1] * (1.0 / math.sqrt(32 * 2048))
    gain_out[...] = jnp.where(half == 0, total[:, :64], total[:, 64:])


def shards(queries, key_rows, value_rows, out_grad, norm_gain, doc_starts):
    q, k, v, dy = (a.reshape(TOK, HEADS * FEAT) for a in (queries, key_rows, value_rows, out_grad))
    starts = doc_starts
    swap = [(i, i ^ 1) for i in range(2 * CHIPS)]
    zgroups = [[2 * z + c for z in range(CHIPS)] for c in range(2)]
    wide = (TOK, HEADS * FEAT)
    half_states = (HALF, FEAT, FEAT)
    mm = 2 * TOK * FEAT * FEAT

    def other(x):
        return lax.ppermute(x, "seq", swap)

    def across(x):
        return lax.all_to_all(x, "seq", 0, 0, axis_index_groups=zgroups, tiled=True)

    part = lax.axis_index("dp")
    row = jnp.where(
        (jnp.arange(8)[:, None] == part // CHIPS) & (jnp.arange(FEAT)[None] // 64 == part % 2),
        jnp.concatenate([norm_gain, norm_gain])[None],
        0.0,
    )
    row = row + lax.ppermute(row, "dp", [(i, i ^ CHIPS) for i in range(4 * CHIPS)])
    keep1, give1 = call(
        state_body, [(half_states, F32)] * 2, 3, 16 * mm, 2 << 20, 1 << 18
    )(starts, k, v)
    recv1 = other(give1)
    (chip,) = call(join_body, [(half_states, F32)], 3, 1 << 18, 3 << 19)(starts, keep1, recv1)
    chip, row, after = lax.optimization_barrier((chip, row, starts))
    parts = across(chip)
    shifted = [
        ((((x ^ (2 * c)) * CHIPS + (y + z) % CHIPS) * CHIPS + z) * 2 + c, ((x * CHIPS + y) * CHIPS + z) * 2 + c)
        for x in range(4) for y in range(CHIPS) for z in range(CHIPS) for c in range(2)
    ]
    gain_rows = lax.ppermute(row, ("dp", "seq"), shifted)
    qf, kf, scores, intra = call(
        local_body, [(wide, BF16)] * 3 + [(wide, F32)], 4, 32 * mm, 4 << 20, 1 << 19, far=True,
        scratch=[pltpu.VMEM(wide, BF16)] * 3 + [pltpu.VMEM(wide, F32), pltpu.SemaphoreType.DMA((16,))],
    )(after, q, k, v)
    parts, scores = lax.optimization_barrier((parts, scores))
    (prefix,) = call(
        scan_body, [((CHIPS, FEAT + 8, FEAT), F32)], 3, 1 << 18, 1 << 20
    )(starts, parts, gain_rows)
    coming = across(prefix)
    (send2,) = call(
        give_body, [((HALF * FEAT + 64, FEAT), F32)], 3, 1 << 18, 3 << 19
    )(starts, keep1, coming)
    ready = other(send2)
    att, dn, inb, keep3, give3, terms = call(
        norm_body,
        [(wide, BF16), (wide, BF16), ((HEADS, FEAT, FEAT), BF16)]
        + [(half_states, F32)] * 2
        + [((64, FEAT), F32)],
        7, 32 * mm, 5 << 20, 1 << 15, scratch=[pltpu.VMEM((64, FEAT), F32)],
    )(starts, qf, intra, dy, coming, recv1, ready)
    lines = [[x * CHIPS + y for y in range(CHIPS)] for x in range(4)]
    gathered = lax.all_to_all(terms, "dp", 0, 0, axis_index_groups=lines, tiled=True)
    recv3 = other(give3)
    (chip3,) = call(join_back_body, [(half_states, F32)], 3, 1 << 18, 3 << 19)(starts, keep3, recv3)
    chip3, gathered, after3 = lax.optimization_barrier((chip3, gathered, starts))
    parts3 = across(chip3)
    total = jnp.sum(gathered.reshape(CHIPS, 8, FEAT), axis=0)
    for step in (2 * CHIPS, CHIPS):
        total = total + lax.ppermute(total, "dp", [(i, i ^ step) for i in range(4 * CHIPS)])
    dq, dk_part, dv_part = call(
        grads_body, [(wide, BF16), (wide, F32), (wide, F32)], 8, 80 * mm, 7 << 20, 1 << 18,
        far=True, far_in=range(1, 8),
        scratch=[pltpu.VMEM(wide, BF16)] * 6
        + [pltpu.VMEM((HEADS, FEAT, FEAT), BF16), pltpu.VMEM(wide, BF16)]
        + [pltpu.VMEM(wide, F32)] * 2
        + [pltpu.SemaphoreType.DMA((40,))],
    )(
        after3,
        *(pltpu.with_memory_space_constraint(x, pltpu.HBM) for x in (q, v, qf, kf, scores, dn, inb)),
    )
    parts3, dk_part = lax.optimization_barrier((parts3, dk_part))
    (suffix,) = call(
        scan_back_body, [((CHIPS, FEAT + 8, FEAT), F32)], 3, 1 << 18, 1 << 20
    )(starts, parts3, total)
    coming4 = across(suffix)
    (send4,) = call(
        give_back_body, [((HALF * FEAT + 8, FEAT), F32)], 3, 1 << 18, 3 << 19
    )(starts, keep3, coming4)
    ready4 = other(send4)
    dk, dv, gain_grad = call(
        last_body, [(wide, BF16)] * 2 + [((1, 64), F32)], 9, 32 * mm, 5 << 20, 1 << 18
    )(starts, k, v, kf, dk_part, dv_part, recv3, coming4, ready4)
    full = (1, TOK, HEADS * FEAT)
    return (
        att.reshape(full),
        dq.reshape(full),
        dk.reshape(full),
        dv.reshape(full),
        gain_grad.reshape(64),
    )


def solution(mesh):
    rows = P("dp", "seq", None)
    return jax.shard_map(
        shards,
        mesh=mesh,
        in_specs=(rows, rows, rows, rows, P("dp"), P("dp", None)),
        out_specs=(rows, rows, rows, rows, P("dp")),
        check_vma=False,
    )
```

```python
import math

import jax
import jax.numpy as jnp
from jax import lax
from jax.experimental import pallas as pl
from jax.experimental.pallas import tpu as pltpu
from jax.sharding import PartitionSpec as P

HEADS = 16
FEAT = 128
TOK = 128
HALF = HEADS // 2
CHIPS = 8
DOCS = 8
EPS = 1e-06
F32 = jnp.float32
BF16 = jnp.bfloat16

VM = pl.BlockSpec(memory_space=pltpu.VMEM)
SM = pl.BlockSpec(memory_space=pltpu.SMEM)
HB = pl.BlockSpec(memory_space=pltpu.HBM)


def call(body, outs, n_in, flops=0, nbytes=0, trans=0, far=False, far_in=(), scratch=()):
    return pl.pallas_call(
        body,
        out_shape=[pltpu.HBM(s, d) if far else jax.ShapeDtypeStruct(s, d) for s, d in outs],
        in_specs=[SM] + [HB if i in far_in else VM for i in range(1, n_in)],
        out_specs=[HB if far else VM] * len(outs),
        scratch_shapes=scratch,
        compiler_params=pltpu.CompilerParams(vmem_limit_bytes=24 * 1024 * 1024),
        cost_estimate=pl.CostEstimate(
            flops=flops, bytes_accessed=nbytes, transcendentals=trans
        ),
    )


def doc_at(starts, p):
    total = jnp.int32(0)
    for j in range(DOCS):
        total = total + (starts[0, j] <= p).astype(jnp.int32)
    return total


def docs_of(starts, pos):
    total = jnp.zeros(pos.shape, jnp.int32)
    for j in range(DOCS):
        total = total + (starts[0, j] <= pos).astype(jnp.int32)
    return total


def place():
    idx = lax.axis_index("seq")
    return idx, lax.rem(idx, 2)


def row_pos(idx):
    return idx * TOK + lax.broadcasted_iota(jnp.int32, (TOK, FEAT), 0)


def enters(starts, idx):
    return docs_of(starts, row_pos(idx)) == doc_at(starts, idx * TOK - 1)


def leaves(starts, idx):
    return docs_of(starts, row_pos(idx)) == doc_at(starts, idx * TOK + TOK - 1)


def mask_of(starts, idx):
    rows = row_pos(idx)
    cols = idx * TOK + lax.broadcasted_iota(jnp.int32, (TOK, TOK), 1)
    return (rows >= cols) & (docs_of(starts, rows) == docs_of(starts, cols))


def carry_of(starts, idx):
    return (doc_at(starts, idx * TOK - 1) == doc_at(starts, idx * TOK + TOK - 1)).astype(F32)


def chip_carry(starts, z):
    first = z * 2 * TOK
    return (doc_at(starts, first - 1) == doc_at(starts, first + 2 * TOK - 1)).astype(F32)


def phi(x):
    return jnp.where(x > 0, x + 1.0, jnp.exp(jnp.minimum(x, 0.0)))


def slope(x):
    return jnp.where(x > 0, 1.0, jnp.exp(jnp.minimum(x, 0.0)))


def dot(a, b, ca, cb):
    return lax.dot_general(a, b, (((ca,), (cb,)), ((), ())), preferred_element_type=F32)


def cols(h):
    return pl.ds(pl.multiple_of(h * FEAT, FEAT), FEAT)


def state_body(starts, k, v, keep, give):
    idx, core = place()
    last = leaves(starts, idx)
    for j in range(HALF):
        for out, side in ((keep, core), (give, 1 - core)):
            at = cols(side * HALF + j)
            kf = jnp.where(last, phi(k[:, at].astype(F32)), 0.0).astype(BF16)
            out[j] = dot(kf, v[:, at], 0, 0)


def join_body(starts, keep, recv, out):
    idx, core = place()
    later = carry_of(starts, idx - core + 1)
    mine = jnp.where(core == 0, later, 1.0)
    theirs = jnp.where(core == 0, 1.0, later)
    for j in range(HALF):
        out[j] = mine * keep[j] + theirs * recv[j]


def join_back_body(starts, keep, recv, out):
    idx, core = place()
    earlier = carry_of(starts, idx - core)
    mine = jnp.where(core == 0, 1.0, earlier)
    theirs = jnp.where(core == 0, earlier, 1.0)
    for j in range(HALF):
        out[j] = mine * keep[j] + theirs * recv[j]


def scan_body(starts, parts, gain_rows, out):
    total = jnp.zeros((FEAT, FEAT), F32)
    for z in range(CHIPS):
        out[z, :FEAT] = total
        out[z, FEAT:] = gain_rows[...]
        if z < CHIPS - 1:
            total = parts[z] + chip_carry(starts, z) * total


def scan_back_body(starts, parts, terms, out):
    total = jnp.zeros((FEAT, FEAT), F32)
    x = lax.axis_index("dp") // CHIPS
    gsum = jnp.broadcast_to(terms[pl.ds(x, 1), :], (8, FEAT))
    for z in reversed(range(CHIPS)):
        out[z, :FEAT] = total
        out[z, FEAT:] = gsum
        if z > 0:
            total = parts[z] + chip_carry(starts, z) * total


def give_body(starts, keep, coming, out):
    idx, core = place()
    flag = carry_of(starts, idx - core)
    a = jnp.where(core == 0, 1.0, 0.0)
    b = jnp.where(core == 0, flag, 1.0)
    for j in range(HALF):
        out[j * FEAT : (j + 1) * FEAT] = a * keep[j] + b * coming[j, :FEAT]
        out[HALF * FEAT + 8 * j : HALF * FEAT + 8 * j + 8] = coming[j, FEAT:]


def give_back_body(starts, keep, coming, out):
    idx, core = place()
    flag = carry_of(starts, idx - core + 1)
    a = jnp.where(core == 0, 0.0, 1.0)
    b = jnp.where(core == 0, 1.0, flag)
    gsum = jnp.zeros((8, FEAT), F32)
    for j in range(HALF):
        out[j * FEAT : (j + 1) * FEAT] = a * keep[j] + b * coming[j, :FEAT]
        gsum = gsum + coming[j, FEAT:]
    out[HALF * FEAT :] = gsum


def local_body(
    starts, q, k, v, qf_out, kf_out, scores_out, intra_out,
    qf_buf, kf_buf, scores_buf, intra_buf, sems,
):
    idx, _ = place()
    mask = mask_of(starts, idx)
    pairs = (
        (qf_buf, qf_out), (kf_buf, kf_out), (scores_buf, scores_out), (intra_buf, intra_out),
    )
    copies = []
    for h in range(HEADS):
        at = slice(h * FEAT, (h + 1) * FEAT)
        qf = phi(q[:, at].astype(F32)).astype(BF16)
        kf = phi(k[:, at].astype(F32)).astype(BF16)
        qf_buf[:, at] = qf
        kf_buf[:, at] = kf
        scores = jnp.where(mask, dot(qf, kf, 1, 1), 0.0).astype(BF16)
        scores_buf[:, at] = scores
        intra_buf[:, at] = dot(scores, v[:, at], 1, 0)
        if h % 4 == 3:
            group = pl.ds((h - 3) * FEAT, 4 * FEAT)
            for n, (buf, out) in enumerate(pairs):
                c = pltpu.make_async_copy(buf.at[:, group], out.at[:, group], sems.at[h - 3 + n])
                c.start()
                copies.append(c)
    for c in copies:
        c.wait()


def norm_body(
    starts, qf, intra, dy, coming, theirs, ready,
    att, dn_out, inb_out, keep, give, terms, gains,
):
    idx, core = place()
    y = lax.rem(lax.axis_index("dp"), CHIPS)
    terms[...] = jnp.zeros_like(terms)
    for j in range(CHIPS):
        at = HALF * FEAT + 8 * j
        gains[8 * j : 8 * j + 8, :] = coming[j, FEAT:] + ready[at : at + 8]
    cin = enters(starts, idx)
    flag = carry_of(starts, idx - core)
    a = jnp.where(core == 0, 0.0, 1.0)
    b = jnp.where(core == 0, 1.0, flag)
    for j in range(HALF):
        for side, state in ((core, keep), (1 - core, give)):
            h = side * HALF + j
            at = cols(h)
            if state is keep:
                incoming = a * theirs[j] + b * coming[j, :FEAT]
            else:
                incoming = ready[j * FEAT : (j + 1) * FEAT]
            inb = incoming.astype(BF16)
            inb_out[h] = inb
            qh = qf[:, at]
            num = intra[:, at] + jnp.where(cin, dot(qh, inb, 1, 0), 0.0)
            recip = lax.rsqrt(jnp.mean(num * num, -1, keepdims=True) + EPS)
            normed = num * recip
            even = lax.rem(2 * lax.rem(h, 4) - y + CHIPS, CHIPS)
            odd = lax.rem(2 * lax.rem(h, 4) + 1 - y + CHIPS, CHIPS)
            gain = gains[pl.ds(8 * even + h // 4, 1), :] + gains[pl.ds(8 * odd + h // 4, 1), :]
            att[:, at] = (normed * gain).astype(BF16)
            grad = dy[:, at].astype(F32)
            upper = grad * gain
            mean = jnp.mean(upper * normed, -1, keepdims=True)
            dn = (recip * upper - normed * recip * mean).astype(BF16)
            dn_out[:, at] = dn
            term = jnp.sum(grad * normed, axis=0, keepdims=True)
            to = 16 * lax.rem(h, 4) + h // 4
            terms[pl.ds(to, 1), :] = term
            terms[pl.ds(to + 8, 1), :] = term
            masked = jnp.where(cin, dn, jnp.zeros_like(dn))
            state[j] = dot(qh, masked, 0, 0)


def grads_body(starts, *refs):
    ins, outs, in_bufs, out_bufs, sems = refs[:7], refs[7:10], refs[10:17], refs[17:20], refs[20]
    q, v, qf, kf, scores, dn, inb = in_bufs
    dq_buf, dk_buf, dv_buf = out_bufs
    groups = [pl.ds(4 * g * FEAT, 4 * FEAT) for g in range(4)]
    coming, going = [], []
    for g in range(4):
        these = []
        for n in range(7):
            if n < 6:
                src, dst = ins[n].at[:, groups[g]], in_bufs[n].at[:, groups[g]]
            else:
                src, dst = ins[n].at[pl.ds(4 * g, 4)], in_bufs[n].at[pl.ds(4 * g, 4)]
            these.append(pltpu.make_async_copy(src, dst, sems.at[10 * g + n]))
        for c in these:
            c.start()
        coming.append(these)
    idx, _ = place()
    mask = mask_of(starts, idx)
    cin = enters(starts, idx)
    for h in range(HEADS):
        g = h // 4
        if h % 4 == 0:
            for c in coming[g]:
                c.wait()
        at = slice(h * FEAT, (h + 1) * FEAT)
        dnh = dn[:, at]
        dscores = jnp.where(mask, dot(dnh, v[:, at], 1, 1), 0.0).astype(BF16)
        dq = dot(dscores, kf[:, at], 1, 0) + jnp.where(cin, dot(dnh, inb[h], 1, 1), 0.0)
        dq_buf[:, at] = (dq * slope(q[:, at].astype(F32))).astype(BF16)
        dk_buf[:, at] = dot(dscores, qf[:, at], 0, 0)
        dv_buf[:, at] = dot(scores[:, at], dnh, 0, 0)
        if h % 4 == 3:
            for n in range(3):
                c = pltpu.make_async_copy(
                    out_bufs[n].at[:, groups[g]], outs[n].at[:, groups[g]], sems.at[10 * g + 7 + n]
                )
                c.start()
                going.append(c)
    for c in going:
        c.wait()


def last_body(
    starts, k, v, kf, dk_part, dv_part, theirs, coming, ready,
    dk_out, dv_out, gain_out,
):
    idx, core = place()
    last = leaves(starts, idx)
    flag = carry_of(starts, idx - core + 1)
    a = jnp.where(core == 0, 1.0, 0.0)
    b = jnp.where(core == 0, flag, 1.0)
    gsum = ready[HALF * FEAT :]
    for j in range(HALF):
        gsum = gsum + coming[j, FEAT:]
        for mine, side in ((True, core), (False, 1 - core)):
            at = cols(side * HALF + j)
            if mine:
                outgoing = a * theirs[j] + b * coming[j, :FEAT]
            else:
                outgoing = ready[j * FEAT : (j + 1) * FEAT]
            outb = outgoing.astype(BF16)
            dk = dk_part[:, at] + jnp.where(last, dot(v[:, at], outb, 1, 1), 0.0)
            dk_out[:, at] = (dk * slope(k[:, at].astype(F32))).astype(BF16)
            dv = dv_part[:, at] + jnp.where(last, dot(kf[:, at], outb, 1, 0), 0.0)
            dv_out[:, at] = dv.astype(BF16)
    half = lax.rem(lax.axis_index("dp"), 2)
    total = gsum[:1] * (1.0 / math.sqrt(32 * 2048))
    gain_out[...] = jnp.where(half == 0, total[:, :64], total[:, 64:])


def shards(queries, key_rows, value_rows, out_grad, norm_gain, doc_starts):
    q, k, v, dy = (a.reshape(TOK, HEADS * FEAT) for a in (queries, key_rows, value_rows, out_grad))
    starts = doc_starts
    swap = [(i, i ^ 1) for i in range(2 * CHIPS)]
    zgroups = [[2 * z + c for z in range(CHIPS)] for c in range(2)]
    wide = (TOK, HEADS * FEAT)
    half_states = (HALF, FEAT, FEAT)
    mm = 2 * TOK * FEAT * FEAT

    def other(x):
        return lax.ppermute(x, "seq", swap)

    def across(x):
        return lax.all_to_all(x, "seq", 0, 0, axis_index_groups=zgroups, tiled=True)

    part = lax.axis_index("dp")
    row = jnp.where(
        (jnp.arange(8)[:, None] == part // CHIPS) & (jnp.arange(FEAT)[None] // 64 == part % 2),
        jnp.concatenate([norm_gain, norm_gain])[None],
        0.0,
    )
    row = row + lax.ppermute(row, "dp", [(i, i ^ CHIPS) for i in range(4 * CHIPS)])
    keep1, give1 = call(
        state_body, [(half_states, F32)] * 2, 3, 16 * mm, 2 << 20, 1 << 18
    )(starts, k, v)
    recv1 = other(give1)
    (chip,) = call(join_body, [(half_states, F32)], 3, 1 << 18, 3 << 19)(starts, keep1, recv1)
    chip, row, after = lax.optimization_barrier((chip, row, starts))
    parts = across(chip)
    shifted = [
        ((((x ^ (2 * c)) * CHIPS + (y + z) % CHIPS) * CHIPS + z) * 2 + c, ((x * CHIPS + y) * CHIPS + z) * 2 + c)
        for x in range(4) for y in range(CHIPS) for z in range(CHIPS) for c in range(2)
    ]
    gain_rows = lax.ppermute(row, ("dp", "seq"), shifted)
    qf, kf, scores, intra = call(
        local_body, [(wide, BF16)] * 3 + [(wide, F32)], 4, 32 * mm, 4 << 20, 1 << 19, far=True,
        scratch=[pltpu.VMEM(wide, BF16)] * 3 + [pltpu.VMEM(wide, F32), pltpu.SemaphoreType.DMA((16,))],
    )(after, q, k, v)
    parts, scores = lax.optimization_barrier((parts, scores))
    (prefix,) = call(
        scan_body, [((CHIPS, FEAT + 8, FEAT), F32)], 3, 1 << 18, 1 << 20
    )(starts, parts, gain_rows)
    coming = across(prefix)
    (send2,) = call(
        give_body, [((HALF * FEAT + 64, FEAT), F32)], 3, 1 << 18, 3 << 19
    )(starts, keep1, coming)
    ready = other(send2)
    att, dn, inb, keep3, give3, terms = call(
        norm_body,
        [(wide, BF16), (wide, BF16), ((HEADS, FEAT, FEAT), BF16)]
        + [(half_states, F32)] * 2
        + [((64, FEAT), F32)],
        7, 32 * mm, 5 << 20, 1 << 15, scratch=[pltpu.VMEM((64, FEAT), F32)],
    )(starts, qf, intra, dy, coming, recv1, ready)
    lines = [[x * CHIPS + y for y in range(CHIPS)] for x in range(4)]
    gathered = lax.all_to_all(terms, "dp", 0, 0, axis_index_groups=lines, tiled=True)
    recv3 = other(give3)
    (chip3,) = call(join_back_body, [(half_states, F32)], 3, 1 << 18, 3 << 19)(starts, keep3, recv3)
    chip3, gathered = lax.optimization_barrier((chip3, gathered))
    parts3 = across(chip3)
    total = jnp.sum(gathered.reshape(CHIPS, 8, FEAT), axis=0)
    for step in (2 * CHIPS, CHIPS):
        total = total + lax.ppermute(total, "dp", [(i, i ^ step) for i in range(4 * CHIPS)])
    (suffix,) = call(
        scan_back_body, [((CHIPS, FEAT + 8, FEAT), F32)], 3, 1 << 18, 1 << 20
    )(starts, parts3, total)
    suffix, after4 = lax.optimization_barrier((suffix, starts))
    coming4 = across(suffix)
    dq, dk_part, dv_part = call(
        grads_body, [(wide, BF16), (wide, F32), (wide, F32)], 8, 80 * mm, 7 << 20, 1 << 18,
        far=True, far_in=range(1, 8),
        scratch=[pltpu.VMEM(wide, BF16)] * 6
        + [pltpu.VMEM((HEADS, FEAT, FEAT), BF16), pltpu.VMEM(wide, BF16)]
        + [pltpu.VMEM(wide, F32)] * 2
        + [pltpu.SemaphoreType.DMA((40,))],
    )(
        after4,
        *(pltpu.with_memory_space_constraint(x, pltpu.HBM) for x in (q, v, qf, kf, scores, dn, inb)),
    )
    coming4, dk_part = lax.optimization_barrier((coming4, dk_part))
    (send4,) = call(
        give_back_body, [((HALF * FEAT + 8, FEAT), F32)], 3, 1 << 18, 3 << 19
    )(starts, keep3, coming4)
    ready4 = other(send4)
    dk, dv, gain_grad = call(
        last_body, [(wide, BF16)] * 2 + [((1, 64), F32)], 9, 32 * mm, 5 << 20, 1 << 18
    )(starts, k, v, kf, dk_part, dv_part, recv3, coming4, ready4)
    full = (1, TOK, HEADS * FEAT)
    return (
        att.reshape(full),
        dq.reshape(full),
        dk.reshape(full),
        dv.reshape(full),
        gain_grad.reshape(64),
    )


def solution(mesh):
    rows = P("dp", "seq", None)
    return jax.shard_map(
        shards,
        mesh=mesh,
        in_specs=(rows, rows, rows, rows, P("dp"), P("dp", None)),
        out_specs=(rows, rows, rows, rows, P("dp")),
        check_vma=False,
    )
```

```python
import math

import jax
import jax.numpy as jnp
from jax import lax
from jax.experimental import pallas as pl
from jax.experimental.pallas import tpu as pltpu
from jax.sharding import PartitionSpec as P

HEADS = 16
FEAT = 128
TOK = 128
HALF = HEADS // 2
CHIPS = 8
DOCS = 8
EPS = 1e-06
F32 = jnp.float32
BF16 = jnp.bfloat16

VM = pl.BlockSpec(memory_space=pltpu.VMEM)
SM = pl.BlockSpec(memory_space=pltpu.SMEM)
HB = pl.BlockSpec(memory_space=pltpu.HBM)


def call(body, outs, n_in, flops=0, nbytes=0, trans=0, far=False, far_in=(), scratch=()):
    return pl.pallas_call(
        body,
        out_shape=[pltpu.HBM(s, d) if far else jax.ShapeDtypeStruct(s, d) for s, d in outs],
        in_specs=[SM] + [HB if i in far_in else VM for i in range(1, n_in)],
        out_specs=[HB if far else VM] * len(outs),
        scratch_shapes=scratch,
        compiler_params=pltpu.CompilerParams(vmem_limit_bytes=24 * 1024 * 1024),
        cost_estimate=pl.CostEstimate(
            flops=flops, bytes_accessed=nbytes, transcendentals=trans
        ),
    )


def doc_at(starts, p):
    total = jnp.int32(0)
    for j in range(DOCS):
        total = total + (starts[0, j] <= p).astype(jnp.int32)
    return total


def docs_of(starts, pos):
    total = jnp.zeros(pos.shape, jnp.int32)
    for j in range(DOCS):
        total = total + (starts[0, j] <= pos).astype(jnp.int32)
    return total


def place():
    idx = lax.axis_index("seq")
    return idx, lax.rem(idx, 2)


def row_pos(idx):
    return idx * TOK + lax.broadcasted_iota(jnp.int32, (TOK, FEAT), 0)


def enters(starts, idx):
    return docs_of(starts, row_pos(idx)) == doc_at(starts, idx * TOK - 1)


def leaves(starts, idx):
    return docs_of(starts, row_pos(idx)) == doc_at(starts, idx * TOK + TOK - 1)


def mask_of(starts, idx):
    rows = row_pos(idx)
    cols = idx * TOK + lax.broadcasted_iota(jnp.int32, (TOK, TOK), 1)
    return (rows >= cols) & (docs_of(starts, rows) == docs_of(starts, cols))


def carry_of(starts, idx):
    return (doc_at(starts, idx * TOK - 1) == doc_at(starts, idx * TOK + TOK - 1)).astype(F32)


def chip_carry(starts, z):
    first = z * 2 * TOK
    return (doc_at(starts, first - 1) == doc_at(starts, first + 2 * TOK - 1)).astype(F32)


def phi(x):
    return jnp.where(x > 0, x + 1.0, jnp.exp(jnp.minimum(x, 0.0)))


def slope(x):
    return jnp.where(x > 0, 1.0, jnp.exp(jnp.minimum(x, 0.0)))


def dot(a, b, ca, cb):
    return lax.dot_general(a, b, (((ca,), (cb,)), ((), ())), preferred_element_type=F32)


def cols(h):
    return pl.ds(pl.multiple_of(h * FEAT, FEAT), FEAT)


def state_body(starts, k, v, keep, give):
    idx, core = place()
    last = leaves(starts, idx)
    for j in range(HALF):
        for out, side in ((keep, core), (give, 1 - core)):
            at = cols(side * HALF + j)
            kf = jnp.where(last, phi(k[:, at].astype(F32)), 0.0).astype(BF16)
            out[j] = dot(kf, v[:, at], 0, 0)


def join_body(starts, keep, recv, out):
    idx, core = place()
    later = carry_of(starts, idx - core + 1)
    mine = jnp.where(core == 0, later, 1.0)
    theirs = jnp.where(core == 0, 1.0, later)
    for j in range(HALF):
        out[j] = mine * keep[j] + theirs * recv[j]


def join_back_body(starts, keep, recv, out):
    idx, core = place()
    earlier = carry_of(starts, idx - core)
    mine = jnp.where(core == 0, 1.0, earlier)
    theirs = jnp.where(core == 0, earlier, 1.0)
    for j in range(HALF):
        out[j] = mine * keep[j] + theirs * recv[j]


def scan_body(starts, parts, gain_rows, out):
    total = jnp.zeros((FEAT, FEAT), F32)
    for z in range(CHIPS):
        out[z, :FEAT] = total
        out[z, FEAT:] = gain_rows[...]
        if z < CHIPS - 1:
            total = parts[z] + chip_carry(starts, z) * total


def scan_back_body(starts, parts, terms, out):
    total = jnp.zeros((FEAT, FEAT), F32)
    x = lax.axis_index("dp") // CHIPS
    gsum = jnp.broadcast_to(terms[pl.ds(x, 1), :], (8, FEAT))
    for z in reversed(range(CHIPS)):
        out[z, :FEAT] = total
        out[z, FEAT:] = gsum
        if z > 0:
            total = parts[z] + chip_carry(starts, z) * total


def give_body(starts, keep, coming, out):
    idx, core = place()
    flag = carry_of(starts, idx - core)
    a = jnp.where(core == 0, 1.0, 0.0)
    b = jnp.where(core == 0, flag, 1.0)
    for j in range(HALF):
        out[j * FEAT : (j + 1) * FEAT] = a * keep[j] + b * coming[j, :FEAT]
        out[HALF * FEAT + 8 * j : HALF * FEAT + 8 * j + 8] = coming[j, FEAT:]


def give_back_body(starts, keep, coming, out):
    idx, core = place()
    flag = carry_of(starts, idx - core + 1)
    a = jnp.where(core == 0, 0.0, 1.0)
    b = jnp.where(core == 0, 1.0, flag)
    gsum = jnp.zeros((8, FEAT), F32)
    for j in range(HALF):
        out[j * FEAT : (j + 1) * FEAT] = a * keep[j] + b * coming[j, :FEAT]
        gsum = gsum + coming[j, FEAT:]
    out[HALF * FEAT :] = gsum


def local_body(
    starts, q, k, v, qf_out, kf_out, scores_out, intra_out,
    qf_buf, kf_buf, scores_buf, intra_buf, sems,
):
    idx, _ = place()
    mask = mask_of(starts, idx)
    pairs = (
        (qf_buf, qf_out), (kf_buf, kf_out), (scores_buf, scores_out), (intra_buf, intra_out),
    )
    copies = []
    for h in range(HEADS):
        at = slice(h * FEAT, (h + 1) * FEAT)
        qf = phi(q[:, at].astype(F32)).astype(BF16)
        kf = phi(k[:, at].astype(F32)).astype(BF16)
        qf_buf[:, at] = qf
        kf_buf[:, at] = kf
        scores = jnp.where(mask, dot(qf, kf, 1, 1), 0.0).astype(BF16)
        scores_buf[:, at] = scores
        intra_buf[:, at] = dot(scores, v[:, at], 1, 0)
        if h % 4 == 3:
            group = pl.ds((h - 3) * FEAT, 4 * FEAT)
            for n, (buf, out) in enumerate(pairs):
                c = pltpu.make_async_copy(buf.at[:, group], out.at[:, group], sems.at[h - 3 + n])
                c.start()
                copies.append(c)
    for c in copies:
        c.wait()


def norm_body(
    starts, qf, intra, dy, coming, theirs, ready,
    att, dn_out, inb_out, keep, give, terms, gains,
):
    idx, core = place()
    y = lax.rem(lax.axis_index("dp"), CHIPS)
    terms[...] = jnp.zeros_like(terms)
    for j in range(CHIPS):
        at = HALF * FEAT + 8 * j
        gains[8 * j : 8 * j + 8, :] = coming[j, FEAT:] + ready[at : at + 8]
    cin = enters(starts, idx)
    flag = carry_of(starts, idx - core)
    a = jnp.where(core == 0, 0.0, 1.0)
    b = jnp.where(core == 0, 1.0, flag)
    for j in range(HALF):
        for side, state in ((core, keep), (1 - core, give)):
            h = side * HALF + j
            at = cols(h)
            if state is keep:
                incoming = a * theirs[j] + b * coming[j, :FEAT]
            else:
                incoming = ready[j * FEAT : (j + 1) * FEAT]
            inb = incoming.astype(BF16)
            inb_out[h] = inb
            qh = qf[:, at]
            num = intra[:, at] + jnp.where(cin, dot(qh, inb, 1, 0), 0.0)
            recip = lax.rsqrt(jnp.mean(num * num, -1, keepdims=True) + EPS)
            normed = num * recip
            even = lax.rem(2 * lax.rem(h, 4) - y + CHIPS, CHIPS)
            odd = lax.rem(2 * lax.rem(h, 4) + 1 - y + CHIPS, CHIPS)
            gain = gains[pl.ds(8 * even + h // 4, 1), :] + gains[pl.ds(8 * odd + h // 4, 1), :]
            att[:, at] = (normed * gain).astype(BF16)
            grad = dy[:, at].astype(F32)
            upper = grad * gain
            mean = jnp.mean(upper * normed, -1, keepdims=True)
            dn = (recip * upper - normed * recip * mean).astype(BF16)
            dn_out[:, at] = dn
            term = jnp.sum(grad * normed, axis=0, keepdims=True)
            to = 16 * lax.rem(h, 4) + h // 4
            terms[pl.ds(to, 1), :] = term
            terms[pl.ds(to + 8, 1), :] = term
            masked = jnp.where(cin, dn, jnp.zeros_like(dn))
            state[j] = dot(qh, masked, 0, 0)


def grads_body(starts, *refs):
    ins, outs, in_bufs, out_bufs, sems = refs[:7], refs[7:10], refs[10:17], refs[17:20], refs[20]
    q, v, qf, kf, scores, dn, inb = in_bufs
    dq_buf, dk_buf, dv_buf = out_bufs
    groups = [pl.ds(4 * g * FEAT, 4 * FEAT) for g in range(4)]
    coming, going = [], []
    for g in range(4):
        these = []
        for n in range(7):
            if n < 6:
                src, dst = ins[n].at[:, groups[g]], in_bufs[n].at[:, groups[g]]
            else:
                src, dst = ins[n].at[pl.ds(4 * g, 4)], in_bufs[n].at[pl.ds(4 * g, 4)]
            these.append(pltpu.make_async_copy(src, dst, sems.at[10 * g + n]))
        for c in these:
            c.start()
        coming.append(these)
    idx, _ = place()
    mask = mask_of(starts, idx)
    cin = enters(starts, idx)
    for h in range(HEADS):
        g = h // 4
        if h % 4 == 0:
            for c in coming[g]:
                c.wait()
        at = slice(h * FEAT, (h + 1) * FEAT)
        dnh = dn[:, at]
        dscores = jnp.where(mask, dot(dnh, v[:, at], 1, 1), 0.0).astype(BF16)
        dq = dot(dscores, kf[:, at], 1, 0) + jnp.where(cin, dot(dnh, inb[h], 1, 1), 0.0)
        dq_buf[:, at] = (dq * slope(q[:, at].astype(F32))).astype(BF16)
        dk_buf[:, at] = dot(dscores, qf[:, at], 0, 0)
        dv_buf[:, at] = dot(scores[:, at], dnh, 0, 0)
        if h % 4 == 3:
            for n in range(3):
                c = pltpu.make_async_copy(
                    out_bufs[n].at[:, groups[g]], outs[n].at[:, groups[g]], sems.at[10 * g + 7 + n]
                )
                c.start()
                going.append(c)
    for c in going:
        c.wait()


def last_body(
    starts, k, v, kf, dk_far, dv_far, theirs, coming, ready,
    dk_out, dv_out, gain_out, dk_part, dv_part, sems,
):
    idx, core = place()
    fetches = []
    for g in range(2):
        these = []
        for n, side in enumerate((core, 1 - core)):
            at = pl.ds(pl.multiple_of((side * HALF + 4 * g) * FEAT, 4 * FEAT), 4 * FEAT)
            for m, (src, dst) in enumerate(((dk_far, dk_part), (dv_far, dv_part))):
                these.append(
                    pltpu.make_async_copy(src.at[:, at], dst.at[:, at], sems.at[4 * g + 2 * n + m])
                )
        for c in these:
            c.start()
        fetches.append(these)
    last = leaves(starts, idx)
    flag = carry_of(starts, idx - core + 1)
    a = jnp.where(core == 0, 1.0, 0.0)
    b = jnp.where(core == 0, flag, 1.0)
    gsum = ready[HALF * FEAT :]
    for j in range(HALF):
        gsum = gsum + coming[j, FEAT:]
        if j % 4 == 0:
            for c in fetches[j // 4]:
                c.wait()
        for mine, side in ((True, core), (False, 1 - core)):
            at = cols(side * HALF + j)
            if mine:
                outgoing = a * theirs[j] + b * coming[j, :FEAT]
            else:
                outgoing = ready[j * FEAT : (j + 1) * FEAT]
            outb = outgoing.astype(BF16)
            dk = dk_part[:, at] + jnp.where(last, dot(v[:, at], outb, 1, 1), 0.0)
            dk_out[:, at] = (dk * slope(k[:, at].astype(F32))).astype(BF16)
            dv = dv_part[:, at] + jnp.where(last, dot(kf[:, at], outb, 1, 0), 0.0)
            dv_out[:, at] = dv.astype(BF16)
    half = lax.rem(lax.axis_index("dp"), 2)
    total = gsum[:1] * (1.0 / math.sqrt(32 * 2048))
    gain_out[...] = jnp.where(half == 0, total[:, :64], total[:, 64:])


def shards(queries, key_rows, value_rows, out_grad, norm_gain, doc_starts):
    q, k, v, dy = (a.reshape(TOK, HEADS * FEAT) for a in (queries, key_rows, value_rows, out_grad))
    starts = doc_starts
    swap = [(i, i ^ 1) for i in range(2 * CHIPS)]
    zgroups = [[2 * z + c for z in range(CHIPS)] for c in range(2)]
    wide = (TOK, HEADS * FEAT)
    half_states = (HALF, FEAT, FEAT)
    mm = 2 * TOK * FEAT * FEAT

    def other(x):
        return lax.ppermute(x, "seq", swap)

    def across(x):
        return lax.all_to_all(x, "seq", 0, 0, axis_index_groups=zgroups, tiled=True)

    part = lax.axis_index("dp")
    row = jnp.where(
        (jnp.arange(8)[:, None] == part // CHIPS) & (jnp.arange(FEAT)[None] // 64 == part % 2),
        jnp.concatenate([norm_gain, norm_gain])[None],
        0.0,
    )
    row = row + lax.ppermute(row, "dp", [(i, i ^ CHIPS) for i in range(4 * CHIPS)])
    keep1, give1 = call(
        state_body, [(half_states, F32)] * 2, 3, 16 * mm, 2 << 20, 1 << 18
    )(starts, k, v)
    recv1 = other(give1)
    (chip,) = call(join_body, [(half_states, F32)], 3, 1 << 18, 3 << 19)(starts, keep1, recv1)
    chip, row, after = lax.optimization_barrier((chip, row, starts))
    parts = across(chip)
    shifted = [
        ((((x ^ (2 * c)) * CHIPS + (y + z) % CHIPS) * CHIPS + z) * 2 + c, ((x * CHIPS + y) * CHIPS + z) * 2 + c)
        for x in range(4) for y in range(CHIPS) for z in range(CHIPS) for c in range(2)
    ]
    gain_rows = lax.ppermute(row, ("dp", "seq"), shifted)
    qf, kf, scores, intra = call(
        local_body, [(wide, BF16)] * 3 + [(wide, F32)], 4, 32 * mm, 4 << 20, 1 << 19, far=True,
        scratch=[pltpu.VMEM(wide, BF16)] * 3 + [pltpu.VMEM(wide, F32), pltpu.SemaphoreType.DMA((16,))],
    )(after, q, k, v)
    parts, scores = lax.optimization_barrier((parts, scores))
    (prefix,) = call(
        scan_body, [((CHIPS, FEAT + 8, FEAT), F32)], 3, 1 << 18, 1 << 20
    )(starts, parts, gain_rows)
    coming = across(prefix)
    (send2,) = call(
        give_body, [((HALF * FEAT + 64, FEAT), F32)], 3, 1 << 18, 3 << 19
    )(starts, keep1, coming)
    ready = other(send2)
    att, dn, inb, keep3, give3, terms = call(
        norm_body,
        [(wide, BF16), (wide, BF16), ((HEADS, FEAT, FEAT), BF16)]
        + [(half_states, F32)] * 2
        + [((64, FEAT), F32)],
        7, 32 * mm, 5 << 20, 1 << 15, scratch=[pltpu.VMEM((64, FEAT), F32)],
    )(starts, qf, intra, dy, coming, recv1, ready)
    lines = [[x * CHIPS + y for y in range(CHIPS)] for x in range(4)]
    gathered = lax.all_to_all(terms, "dp", 0, 0, axis_index_groups=lines, tiled=True)
    recv3 = other(give3)
    (chip3,) = call(join_back_body, [(half_states, F32)], 3, 1 << 18, 3 << 19)(starts, keep3, recv3)
    chip3, gathered = lax.optimization_barrier((chip3, gathered))
    parts3 = across(chip3)
    total = jnp.sum(gathered.reshape(CHIPS, 8, FEAT), axis=0)
    for step in (2 * CHIPS, CHIPS):
        total = total + lax.ppermute(total, "dp", [(i, i ^ step) for i in range(4 * CHIPS)])
    (suffix,) = call(
        scan_back_body, [((CHIPS, FEAT + 8, FEAT), F32)], 3, 1 << 18, 1 << 20
    )(starts, parts3, total)
    suffix, after4 = lax.optimization_barrier((suffix, starts))
    coming4 = across(suffix)
    dq, dk_part, dv_part = call(
        grads_body, [(wide, BF16), (wide, F32), (wide, F32)], 8, 80 * mm, 7 << 20, 1 << 18,
        far=True, far_in=range(1, 8),
        scratch=[pltpu.VMEM(wide, BF16)] * 6
        + [pltpu.VMEM((HEADS, FEAT, FEAT), BF16), pltpu.VMEM(wide, BF16)]
        + [pltpu.VMEM(wide, F32)] * 2
        + [pltpu.SemaphoreType.DMA((40,))],
    )(
        after4,
        *(pltpu.with_memory_space_constraint(x, pltpu.HBM) for x in (q, v, qf, kf, scores, dn, inb)),
    )
    coming4, dk_part = lax.optimization_barrier((coming4, dk_part))
    (send4,) = call(
        give_back_body, [((HALF * FEAT + 8, FEAT), F32)], 3, 1 << 18, 3 << 19
    )(starts, keep3, coming4)
    ready4 = other(send4)
    dk, dv, gain_grad = call(
        last_body, [(wide, BF16)] * 2 + [((1, 64), F32)], 9, 32 * mm, 5 << 20, 1 << 18,
        far_in=(4, 5), scratch=[pltpu.VMEM(wide, F32)] * 2 + [pltpu.SemaphoreType.DMA((8,))],
    )(
        starts, k, v, kf,
        *(pltpu.with_memory_space_constraint(x, pltpu.HBM) for x in (dk_part, dv_part)),
        recv3, coming4, ready4,
    )
    full = (1, TOK, HEADS * FEAT)
    return (
        att.reshape(full),
        dq.reshape(full),
        dk.reshape(full),
        dv.reshape(full),
        gain_grad.reshape(64),
    )


def solution(mesh):
    rows = P("dp", "seq", None)
    return jax.shard_map(
        shards,
        mesh=mesh,
        in_specs=(rows, rows, rows, rows, P("dp"), P("dp", None)),
        out_specs=(rows, rows, rows, rows, P("dp")),
        check_vma=False,
    )
```
